128 devices in a mesh: section: 8 (over y, core), perim: 16 (over z, x).
Axes of the slice: x: 4, y: 4, z: 4, core: 2. Of those that a mesh axis runs over, the one named last changes fastest.
Arguments:
- radiosity: float32 [8, 16, 128, 256], P(None, 'section', 'perim'), may hold values from -6 to 6
- emission: float32 [8, 16, 128, 256], P(None, 'section', 'perim'), may hold values from -6 to 6
- reflect: float32 [8, 16, 128, 256], P(None, 'section', 'perim'), may hold values from 0.3 to 0.9
- basis: bfloat16 [16, 128, 64, 256], P('section', 'perim'), may hold values from -0.375 to 0.375
- up_leaf: bfloat16 [16, 128, 64, 64], P('section', 'perim'), may hold values from -0.5 to 0.5
- upward_pair_transfer: bfloat16 [8, 128, 64, 64], P('section', 'perim'), may hold values from -0.25 to 0.25
- near_block: bfloat16 [16, 128, 6, 256, 256], P('section', 'perim'), may hold values from -0.15625 to 0.15625
- couple_leaf: bfloat16 [16, 128, 64, 1024], P('section', 'perim'), may hold values from -0.1875 to 0.1875
- couple_pair: bfloat16 [8, 128, 64, 1024], P('section', 'perim'), may hold values from -0.1875 to 0.1875
- couple_top: bfloat16 [8, 16, 64, 512], P('section', 'perim'), may hold values from -0.25 to 0.25
- near_list: int32 [16, 128, 6], P('section', 'perim'), may hold values from 0 to 2047, as said below
- far_leaf: int32 [16, 128, 16], P('section', 'perim'), may hold values from 0 to 2047, as said below
- far_pair: int32 [8, 128, 16], P('section', 'perim'), may hold values from 0 to 1023, as said below
- far_top: int32 [8, 16, 8], P('section', 'perim'), may hold values from 0 to 127, as said below
Outputs:
- radiosity_next: float32 [8, 16, 128, 256], P(None, 'section', 'perim')
The draws below stay inside these ranges and needn't reach their ends.
Inputs may be any that keep to these rules, and one draw needn't show every extreme that they name: `near_list`: entry n > 0 names a leaf whose row differs by at most one (clipped to the tower) and whose column differs by at most one around the perimeter, which closes; entry 0 is the leaf itself. `far_leaf`: A partner leaf lies in a leaf row of the same device row (row // 2) as the leaf or of the one above or below, and two or more columns away around the perimeter. `far_pair`: A partner pair cluster lies in the same pair row or the one above or below, two or more columns away around the perimeter. `far_top`: A partner top cluster lies two or more pair rows away in height.
All inputs are finite; a program needn't handle non-finite values.
Results may differ from the reference program's by a relative error of at most 0.0023.
Values may be sent and summed in bfloat16 or wider, within the bound.
No kernel may reach another device: no remote copies, remote signals or barrier semaphores. Data moves between devices by JAX's collectives and lax.ppermute only.
A program may use at most 64 MiB of HBM per device.

```python
import math
import jax
import jax.numpy as jnp
from jax import lax

LEAF = 256
RANK = 64
BANDS = 8
NEAR = 6
FAR0 = 16
FAR1 = 16
FAR2 = 8
LS = 2
LP = 8
GS = 16
GP = 128
PAIR_ROWS = 8
TOP_COLS = 16


def draw_near_list(key, part):
    key = jax.random.fold_in(key, 11)
    rows = jnp.arange(GS, dtype=jnp.int32)[:, None, None]
    cols = jnp.arange(GP, dtype=jnp.int32)[None, :, None]
    scores = jax.random.randint(key, (GS, GP, 8), 0, 1 << 20) * 8 + jnp.arange(8, dtype=jnp.int32)
    order = jnp.argsort(scores, axis=-1)[..., :NEAR - 1]
    rise_table = jnp.array([-1, -1, -1, 0, 0, 1, 1, 1], jnp.int32)
    turn_table = jnp.array([-1, 0, 1, -1, 1, -1, 0, 1], jnp.int32)
    target_rows = jnp.clip(rows + rise_table[order], 0, GS - 1)
    target_cols = (cols + turn_table[order]) % GP
    others = target_rows * GP + target_cols
    itself = jnp.broadcast_to(rows * GP + cols, (GS, GP, 1))
    return jnp.concatenate([itself, others], axis=-1).astype(jnp.int32)


def draw_far_leaf(key, part):
    key = jax.random.fold_in(key, 12)
    first, second, third = jax.random.split(key, 3)
    rows = jnp.arange(GS, dtype=jnp.int32)[:, None, None]
    cols = jnp.arange(GP, dtype=jnp.int32)[None, :, None]
    target_sec = jnp.clip(rows // LS + jax.random.randint(first, (GS, GP, FAR0), -1, 2), 0, GS // LS - 1)
    target_rows = target_sec * LS + jax.random.randint(second, (GS, GP, FAR0), 0, LS)
    target_cols = (cols + jax.random.randint(third, (GS, GP, FAR0), 2, GP - 1)) % GP
    return (target_rows * GP + target_cols).astype(jnp.int32)


def draw_far_pair(key, part):
    key = jax.random.fold_in(key, 13)
    first, second = jax.random.split(key, 2)
    rows = jnp.arange(PAIR_ROWS, dtype=jnp.int32)[:, None, None]
    cols = jnp.arange(GP, dtype=jnp.int32)[None, :, None]
    target_rows = jnp.clip(rows + jax.random.randint(first, (PAIR_ROWS, GP, FAR1), -1, 2), 0, PAIR_ROWS - 1)
    target_cols = (cols + jax.random.randint(second, (PAIR_ROWS, GP, FAR1), 2, GP - 1)) % GP
    return (target_rows * GP + target_cols).astype(jnp.int32)


def draw_far_top(key, part):
    key = jax.random.fold_in(key, 14)
    first, second = jax.random.split(key, 2)
    rows = jnp.arange(PAIR_ROWS, dtype=jnp.int32)[:, None, None]
    target_rows = (rows + jax.random.randint(first, (PAIR_ROWS, TOP_COLS, FAR2), 2, PAIR_ROWS - 1)) % PAIR_ROWS
    target_cols = jax.random.randint(second, (PAIR_ROWS, TOP_COLS, FAR2), 0, TOP_COLS)
    return (target_rows * TOP_COLS + target_cols).astype(jnp.int32)


def steps_of(stream_key, shape, cuts, least, high):
    level = 1.0
    for axis_at, blocks in cuts:
        draws = jax.random.uniform(jax.random.fold_in(jax.random.fold_in(stream_key, 6), axis_at), (blocks,), jnp.float32, least / len(cuts), high / len(cuts))
        level = level * jnp.repeat(jnp.exp(draws), shape[axis_at] // blocks).reshape((-1,) + (1,) * (len(shape) - 1 - axis_at))
    return level


def gaussian(own_key, dims, deviation, bound, cuts=(), kind=jnp.bfloat16):
    result = jax.random.normal(own_key, dims, jnp.float32) * deviation
    if len(cuts) > 0:
        result = steps_of(own_key, dims, cuts, -0.22, 0.18) * result
    return jnp.clip(result, min=-bound, max=bound).astype(kind)


def setup_inputs(seed: int = 0) -> dict:
    arg_keys = jax.random.split(jax.random.key(seed), 15)
    radiosity = gaussian(arg_keys[0], (BANDS, GS, GP, LEAF), 1.0, 6.0, ((1, 8), (2, 16)), jnp.float32)
    emission = gaussian(arg_keys[1], (BANDS, GS, GP, LEAF), 1.0, 6.0, ((1, 8), (2, 16)), jnp.float32)
    reflect = jnp.clip(jnp.exp(math.log(0.9) - 1.0986122 * jax.random.uniform(arg_keys[2], (BANDS, GS, GP, LEAF), jnp.float32) ** steps_of(arg_keys[2], (BANDS, GS, GP, LEAF), ((1, 8), (2, 16)), -0.2, 0.2)), 0.3, 0.9)
    basis = gaussian(arg_keys[3], (GS, GP, RANK, LEAF), LEAF ** -0.5, 0.375, ((0, 8), (1, 16)))
    up_leaf = gaussian(arg_keys[4], (GS, GP, RANK, RANK), (2 * RANK) ** -0.5, 0.5, ((0, 8), (1, 16)))
    upward_pair_transfer = gaussian(arg_keys[5], (PAIR_ROWS, GP, RANK, RANK), (LP * RANK) ** -0.5, 0.25, ((0, 8), (1, 16)))
    near_block = gaussian(arg_keys[6], (GS, GP, NEAR, LEAF, LEAF), (NEAR * LEAF) ** -0.5, 0.15625, ((0, 8), (1, 16)))
    couple_leaf = gaussian(arg_keys[7], (GS, GP, RANK, FAR0 * RANK), (FAR0 * RANK) ** -0.5, 0.1875, ((0, 8), (1, 16)))
    couple_pair = gaussian(arg_keys[8], (PAIR_ROWS, GP, RANK, FAR1 * RANK), (FAR1 * RANK) ** -0.5, 0.1875, ((0, 8), (1, 16)))
    couple_top = gaussian(arg_keys[9], (PAIR_ROWS, TOP_COLS, RANK, FAR2 * RANK), (FAR2 * RANK) ** -0.5, 0.25, ((0, 8), (1, 16)))
    near_list = draw_near_list(jax.random.fold_in(arg_keys[14], 71), 0)
    far_leaf = draw_far_leaf(jax.random.fold_in(arg_keys[14], 71), 0)
    far_pair = draw_far_pair(jax.random.fold_in(arg_keys[14], 71), 0)
    far_top = draw_far_top(jax.random.fold_in(arg_keys[14], 71), 0)
    return dict(radiosity=radiosity, emission=emission, reflect=reflect, basis=basis, up_leaf=up_leaf, upward_pair_transfer=upward_pair_transfer, near_block=near_block, couple_leaf=couple_leaf, couple_pair=couple_pair, couple_top=couple_top, near_list=near_list, far_leaf=far_leaf, far_pair=far_pair, far_top=far_top)


def rounded(value):
    return lax.optimization_barrier(value.astype(jnp.bfloat16)).astype(jnp.float32)


def reference(radiosity, emission, reflect, basis, up_leaf, upward_pair_transfer, near_block, couple_leaf, couple_pair, couple_top, near_list, far_leaf, far_pair, far_top):
    shaded = radiosity.astype(jnp.bfloat16)
    flat = shaded.reshape(BANDS, GS * GP, LEAF)

    def near_row(row):
        blocks, listed = row
        taken = flat[:, listed].astype(jnp.float32)
        return jnp.einsum("pnij,bpnj->bpi", blocks.astype(jnp.float32), taken)

    nearby_portion = jnp.transpose(lax.map(near_row, (near_block, near_list)), (1, 0, 2, 3))
    shaded_wide = rounded(radiosity)
    leaf_coef = jnp.einsum("xlrj,bxlj->xlrb", basis.astype(jnp.float32), shaded_wide).astype(jnp.bfloat16)
    leaf_quintet = up_leaf.astype(jnp.float32).reshape(PAIR_ROWS, LS, GP, RANK, RANK)
    pair_coefficient = jnp.einsum("xclsr,xclsb->xlrb", leaf_quintet, leaf_coef.astype(jnp.float32).reshape(PAIR_ROWS, LS, GP, RANK, BANDS)).astype(jnp.bfloat16)
    pair_five = upward_pair_transfer.astype(jnp.float32).reshape(PAIR_ROWS, TOP_COLS, LP, RANK, RANK)
    top_coef = jnp.einsum("xplsr,xplsb->xprb", pair_five, pair_coefficient.astype(jnp.float32).reshape(PAIR_ROWS, TOP_COLS, LP, RANK, BANDS)).astype(jnp.bfloat16)
    leaf_pick = leaf_coef.reshape(GS * GP, RANK, BANDS)[far_leaf].reshape(GS, GP, FAR0 * RANK, BANDS)
    leaf_radiosity_field = jnp.einsum("xlrc,xlcb->xlrb", couple_leaf.astype(jnp.float32), leaf_pick.astype(jnp.float32))
    pair_pick = pair_coefficient.reshape(PAIR_ROWS * GP, RANK, BANDS)[far_pair].reshape(PAIR_ROWS, GP, FAR1 * RANK, BANDS)
    pair_radiosity_field = jnp.einsum("xlrc,xlcb->xlrb", couple_pair.astype(jnp.float32), pair_pick.astype(jnp.float32))
    top_pick = top_coef.reshape(PAIR_ROWS * TOP_COLS, RANK, BANDS)[far_top].reshape(PAIR_ROWS, TOP_COLS, FAR2 * RANK, BANDS)
    top_field = jnp.einsum("xprc,xpcb->xprb", couple_top.astype(jnp.float32), top_pick.astype(jnp.float32))
    pair_total = pair_radiosity_field + jnp.einsum("xplsr,xprb->xplsb", pair_five, rounded(top_field)).reshape(PAIR_ROWS, GP, RANK, BANDS)
    leaf_total = leaf_radiosity_field + jnp.einsum("xclsr,xlrb->xclsb", leaf_quintet, rounded(pair_total)).reshape(GS, GP, RANK, BANDS)
    far_part = jnp.einsum("xlrj,xlrb->bxlj", basis.astype(jnp.float32), rounded(leaf_total))
    return emission + reflect * (nearby_portion + far_part)
```

```python
import jax
import jax.numpy as jnp
from jax import lax
from jax.experimental import pallas as pl
from jax.experimental.pallas import tpu as pltpu
from jax.sharding import PartitionSpec as P

F32 = jnp.float32
BF16 = jnp.bfloat16
NT = (((1,), (1,)), ((), ()))
NN = (((1,), (0,)), ((), ()))
LANES = 128
RANK = 64
WIDE = 1152
VMEM = pl.BlockSpec(memory_space=pltpu.VMEM)
SMEM = pl.BlockSpec(memory_space=pltpu.SMEM)


def dot(left, right, dims):
    return lax.dot_general(left, right, dims, preferred_element_type=F32)


def row_of(shape, count):
    return lax.broadcasted_iota(jnp.int32, shape, 0) % count


def own_blocks(products, count):
    shape = (products.shape[0], LANES)
    mine = row_of(shape, count) - lax.broadcasted_iota(jnp.int32, shape, 1) // RANK
    total = jnp.zeros(shape, F32)
    for tile in range(count // 2):
        total += jnp.where(mine == 2 * tile, products[:, tile * LANES : (tile + 1) * LANES], 0.0)
    return total + pltpu.roll(total, RANK, 1)


def side_by_side(twice, count):
    low = lax.broadcasted_iota(jnp.int32, (count, LANES), 1) < RANK
    return jnp.concatenate(
        [
            jnp.where(low, twice[b * count : (b + 1) * count], twice[(b + 1) * count : (b + 2) * count])
            for b in range(0, twice.shape[0] // count, 2)
        ],
        axis=1,
    )


def coefficients_kernel(
    place, radiosity, basis, up_leaf, up_pair, sent, cells, to_mate, to_other
):
    section, column = place[0], place[1]
    bands, rows, cols, leaf = radiosity.shape
    leaves = rows * cols
    for g in range(rows):
        turned = jnp.swapaxes(radiosity[:, g], 0, 1)
        cells[g * cols : (g + 1) * cols] = turned.astype(BF16)
    odd = section % 2
    for g in range(rows):
        row = cells[g * cols : (g + 1) * cols]

        @pl.when(odd == g)
        def _():
            to_other[...] = row

        @pl.when(odd != g)
        def _():
            to_mate[...] = row

    shaded = radiosity[...].reshape(bands * leaves, leaf).astype(BF16)
    leaf_twice = own_blocks(dot(shaded, basis[...], NT), leaves)
    leaf_coef = leaf_twice[:, :RANK].astype(BF16)
    parts = jnp.zeros((bands * leaves, RANK), F32)
    which = row_of(parts.shape, leaves)
    for at in range(leaves):
        parts += jnp.where(which == at, dot(leaf_coef, up_leaf[at], NN), 0.0)
    pair = jnp.sum(parts.reshape(bands, rows, cols, RANK), axis=1).reshape(bands * cols, RANK)
    pair_coef = pair.astype(BF16)
    parts = jnp.zeros((bands * cols, RANK), F32)
    which = row_of(parts.shape, cols)
    for at in range(cols):
        parts += jnp.where(which == at, dot(pair_coef, up_pair[at], NN), 0.0)
    top = jnp.sum(parts.reshape(bands, cols, RANK), axis=1)
    top_twice = jnp.concatenate([top, top], axis=1)
    pair_twice = jnp.concatenate([pair, pair], axis=1)

    def edge(col):
        return jnp.concatenate(
            [radiosity[:, g, col, :] for g in range(rows)], axis=1
        )

    leaf_part = side_by_side(leaf_twice, leaves)
    pair_part = side_by_side(pair_twice, cols)
    top_part = jnp.concatenate([top_twice, jnp.zeros_like(top_twice)], axis=0)

    def block(col):
        return jnp.concatenate(
            [leaf_part, jnp.concatenate([pair_part, edge(col)], axis=0), top_part], axis=1
        ).astype(BF16)

    first = block(0)
    for to in range(sent.shape[0]):
        sent[to] = first
    sent[(column + 1) % sent.shape[0]] = block(cols - 1)


def near_kernel(
    place, listed, cells, from_mate, from_other, ring, ring_mate, ring_other, blocks, out, window
):
    section, column = place[0], place[1]
    step = pl.program_id(0)
    cols = from_mate.shape[0]
    leaf = cells.shape[-1]
    around = ring.shape[0]
    broad = cols + 2

    @pl.when(step == 0)
    def _():
        odd = section % 2
        left = (column + around - 1) % around
        right = (column + 1) % around

        def edges(source, g, at):
            start = at * broad
            lanes = slice(512 + g * leaf, 512 + (g + 1) * leaf)
            window[start] = source[left, 8:16, lanes].astype(F32)
            window[start + broad - 1] = source[right, 8:16, lanes].astype(F32)

        for g in range(2):
            start = (g + 1) * broad + 1
            window[start : start + cols] = cells[g * cols : (g + 1) * cols].astype(F32)
            edges(ring, g, g + 1)

        @pl.when(odd == 0)
        def _():
            window[1 : 1 + cols] = from_other[...].astype(F32)
            window[3 * broad + 1 : 3 * broad + 1 + cols] = from_mate[...].astype(F32)
            edges(ring_other, 1, 0)
            edges(ring_mate, 0, 3)

        @pl.when(odd == 1)
        def _():
            window[1 : 1 + cols] = from_mate[...].astype(F32)
            window[3 * broad + 1 : 3 * broad + 1 + cols] = from_other[...].astype(F32)
            edges(ring_mate, 1, 0)
            edges(ring_other, 0, 3)

    count = blocks.shape[1]
    width_all = around * cols
    total = jnp.zeros(out.shape[1:], F32)
    for n in range(count):
        name = listed[step * count + n]
        up = name // width_all - 2 * section + 1
        turn = (name % width_all + width_all + 1 - cols * column) % width_all
        seen = window[up * broad + turn].astype(BF16)
        total += dot(seen, blocks[0, n], NT)
    out[0] = total


def chosen(tables, lanes, tier, inner, count):
    size = tables[0].shape[0] * tables[0].shape[1]
    picks = inner.shape[1]
    result = jnp.zeros((count * picks, 512), F32)
    at = lax.broadcasted_iota(jnp.int32, (count, size), 1)
    for number, table in enumerate(tables):
        slots = jnp.where(tier == number, inner, -1)
        choose = jnp.concatenate(
            [(at == slots[:, k : k + 1]).astype(F32) for k in range(picks)], axis=0
        ).astype(BF16)
        result += dot(choose, table[:, :, lanes].reshape(size, 512), NN)
    low = lax.broadcasted_iota(jnp.int32, (count, LANES), 1) < RANK
    bands = []
    for n in range(4):
        even, odd = [], []
        for k in range(0, picks, 2):
            one = result[k * count : (k + 1) * count, n * LANES : (n + 1) * LANES]
            two = result[(k + 1) * count : (k + 2) * count, n * LANES : (n + 1) * LANES]
            even.append(jnp.where(low, one, pltpu.roll(two, RANK, 1)))
            odd.append(jnp.where(low, pltpu.roll(one, RANK, 1), two))
        bands += [jnp.concatenate(even, axis=1), jnp.concatenate(odd, axis=1)]
    return jnp.concatenate(bands, axis=0).astype(BF16)


def far_kernel(
    place,
    far_top,
    far_leaf,
    far_pair,
    ring,
    ring_mate,
    ring_other,
    tops,
    couple_leaf,
    couple_pair,
    couple_top,
    basis,
    up_leaf,
    up_pair,
    near,
    emission,
    reflect,
    out,
):
    section = place[0]
    mate = section + 1 - 2 * (section % 2)
    bands, rows, cols, leaf = out.shape
    leaves = rows * cols
    around = ring.shape[0]
    width_all = around * cols
    tables = (ring, ring_mate, ring_other)

    def tier_of(source):
        return jnp.where(source == section, 0, jnp.where(source == mate, 1, 2))

    names = far_leaf[...]
    turn = names % width_all
    height = names // width_all
    leaf_pick = chosen(
        tables,
        slice(0, 512),
        tier_of(height // rows),
        turn // cols * leaves + height % rows * cols + turn % cols,
        leaves,
    )
    leaf_field = own_blocks(dot(leaf_pick, couple_leaf[...], NT), leaves)[:, :RANK]
    names = far_pair[...]
    turn = names % width_all
    pair_pick = chosen(
        tables,
        slice(512, 1024),
        tier_of(names // width_all),
        turn // cols * leaves + turn % cols,
        cols,
    )
    pair_field = own_blocks(dot(pair_pick, couple_pair[...], NT), cols)[:, :RANK]
    top_pick = jnp.concatenate(
        [tops[far_top[k]][:, :RANK].astype(F32) for k in range(far_top.shape[0])], axis=1
    ).astype(BF16)
    top_field = dot(top_pick, couple_top[...], NT)
    spread = jnp.broadcast_to(top_field[:, None, :], (bands, cols, RANK))
    spread = spread.reshape(bands * cols, RANK).astype(BF16)
    pair_total = pair_field + own_blocks(dot(spread, up_pair[...], NT), cols)[:, :RANK]
    spread = jnp.broadcast_to(
        pair_total.reshape(bands, 1, cols, RANK), (bands, rows, cols, RANK)
    )
    spread = spread.reshape(bands * leaves, RANK).astype(BF16)
    leaf_total = leaf_field + own_blocks(dot(spread, up_leaf[...], NT), leaves)[:, :RANK]
    leaf_total = leaf_total.astype(BF16)
    far_part = jnp.zeros((bands * leaves, leaf), F32)
    which = row_of(far_part.shape, leaves)
    for at in range(leaves):
        far_part += jnp.where(which == at, dot(leaf_total, basis[at], NN), 0.0)
    far_part = far_part.reshape(bands, rows, cols, leaf)
    for g in range(rows):
        near_part = jnp.swapaxes(near[g * cols : (g + 1) * cols], 0, 1)
        out[:, g] = emission[:, g] + reflect[:, g] * (near_part + far_part[:, g])


def body(
    radiosity,
    emission,
    reflect,
    basis,
    up_leaf,
    upward_pair_transfer,
    near_block,
    couple_leaf,
    couple_pair,
    couple_top,
    near_list,
    far_leaf,
    far_pair,
    far_top,
):
    around = lax.axis_size("perim")
    tall = lax.axis_size("section")
    bands, rows, cols, leaf = radiosity.shape
    leaves = rows * cols
    place = jnp.stack([lax.axis_index("section"), lax.axis_index("perim")]).astype(jnp.int32)
    mates = [(s, s ^ 1) for s in range(tall)]
    others = [(s, s + 1 if s % 2 else s - 1) for s in range(1, tall - 1)]
    params = pltpu.CompilerParams(vmem_limit_bytes=40 * 1024 * 1024)
    sent, cells, to_mate, to_other = pl.pallas_call(
        coefficients_kernel,
        out_shape=[
            jax.ShapeDtypeStruct((around, 16, WIDE), BF16),
            jax.ShapeDtypeStruct((leaves, bands, leaf), BF16),
            jax.ShapeDtypeStruct((cols, bands, leaf), BF16),
            jax.ShapeDtypeStruct((cols, bands, leaf), BF16),
        ],
        in_specs=[SMEM, VMEM, VMEM, VMEM, VMEM],
        out_specs=[VMEM] * 4,
        compiler_params=params,
        name="coefficients",
    )(
        place,
        radiosity,
        basis.reshape(leaves * RANK, leaf),
        up_leaf.reshape(leaves, RANK, RANK),
        upward_pair_transfer[0],
    )
    from_mate = lax.ppermute(to_mate, "section", mates)
    from_other = lax.ppermute(to_other, "section", others)
    ring = lax.all_to_all(sent, "perim", 0, 0)
    ring_mate = lax.ppermute(ring, "section", mates)
    ring_other = lax.ppermute(ring, "section", others)
    tops = ring[:, :bands, 1024:]
    tops = lax.all_to_all(jnp.broadcast_to(tops[None], (tall,) + tops.shape), "section", 0, 0)
    near = pl.pallas_call(
        near_kernel,
        grid=(leaves,),
        out_shape=jax.ShapeDtypeStruct((leaves, bands, leaf), F32),
        in_specs=[SMEM, SMEM] + [VMEM] * 6
        + [pl.BlockSpec((1,) + near_block.shape[2:], lambda i: (i, 0, 0, 0))],
        out_specs=pl.BlockSpec((1, bands, leaf), lambda i: (i, 0, 0)),
        scratch_shapes=[pltpu.VMEM(((rows + 2) * (cols + 2), bands, leaf), F32)],
        compiler_params=params,
        name="near",
    )(
        place,
        near_list.reshape(-1),
        cells,
        from_mate,
        from_other,
        ring,
        ring_mate,
        ring_other,
        near_block.reshape((leaves,) + near_block.shape[2:]),
    )
    return pl.pallas_call(
        far_kernel,
        out_shape=jax.ShapeDtypeStruct(radiosity.shape, F32),
        in_specs=[SMEM, SMEM] + [VMEM] * 15,
        out_specs=VMEM,
        compiler_params=params,
        name="far",
    )(
        place,
        far_top.reshape(-1),
        far_leaf.reshape(leaves, -1),
        far_pair.reshape(cols, -1),
        ring,
        ring_mate,
        ring_other,
        tops.reshape(tall * around, bands, LANES),
        couple_leaf.reshape(leaves * RANK, -1),
        couple_pair.reshape(cols * RANK, -1),
        couple_top[0, 0],
        basis.reshape(leaves, RANK, leaf),
        up_leaf.reshape(leaves * RANK, RANK),
        upward_pair_transfer.reshape(cols * RANK, RANK),
        near,
        emission,
        reflect,
    )


def solution(mesh):
    cells = P(None, "section", "perim", None)
    four = P("section", "perim", None, None)
    lists = P("section", "perim", None)
    return jax.shard_map(
        body,
        mesh=mesh,
        in_specs=(cells,) * 3
        + (four,) * 3
        + (P("section", "perim", None, None, None),)
        + (four,) * 3
        + (lists,) * 4,
        out_specs=cells,
        check_vma=False,
    )
```

```python
import jax
import jax.numpy as jnp
from jax import lax
from jax.experimental import pallas as pl
from jax.experimental.pallas import tpu as pltpu
from jax.sharding import PartitionSpec as P

F32 = jnp.float32
BF16 = jnp.bfloat16
NT = (((1,), (1,)), ((), ()))
NN = (((1,), (0,)), ((), ()))
LANES = 128
RANK = 64
WIDE = 1152
VMEM = pl.BlockSpec(memory_space=pltpu.VMEM)
SMEM = pl.BlockSpec(memory_space=pltpu.SMEM)
HBM = pl.BlockSpec(memory_space=pltpu.HBM)


def dot(left, right, dims):
    return lax.dot_general(left, right, dims, preferred_element_type=F32)


def far(x):
    return pltpu.with_memory_space_constraint(x, pltpu.HBM)


def limit(mib):
    return pltpu.CompilerParams(vmem_limit_bytes=mib * 1024 * 1024)


def row_of(shape, count):
    return lax.broadcasted_iota(jnp.int32, shape, 0) % count


def own_blocks(products, count):
    shape = (products.shape[0], LANES)
    mine = row_of(shape, count) - lax.broadcasted_iota(jnp.int32, shape, 1) // RANK
    total = jnp.zeros(shape, F32)
    for tile in range(count // 2):
        total += jnp.where(mine == 2 * tile, products[:, tile * LANES : (tile + 1) * LANES], 0.0)
    return total + pltpu.roll(total, RANK, 1)


def side_by_side(twice, count):
    low = lax.broadcasted_iota(jnp.int32, (count, LANES), 1) < RANK
    return jnp.concatenate(
        [
            jnp.where(low, twice[b * count : (b + 1) * count], twice[(b + 1) * count : (b + 2) * count])
            for b in range(0, twice.shape[0] // count, 2)
        ],
        axis=1,
    )


def started(copies, sems, at=0):
    made = []
    for number, (source, target) in enumerate(copies):
        made.append(pltpu.make_async_copy(source, target, sems.at[at + number]))
        made[-1].start()
    return made


def coefficients_kernel(
    place,
    far_radiosity,
    far_basis,
    far_up_leaf,
    far_up_pair,
    sent,
    cells,
    radiosity,
    basis,
    up_leaf,
    up_pair,
    sems,
):
    copies = started(
        [
            (far_radiosity, radiosity),
            (far_basis, basis),
            (far_up_leaf, up_leaf),
            (far_up_pair, up_pair),
        ],
        sems,
    )
    copies[0].wait()
    column = place[1]
    bands, rows, cols, leaf = radiosity.shape
    leaves = rows * cols
    for g in range(rows):
        turned = jnp.swapaxes(radiosity[:, g], 0, 1)
        cells[g * cols : (g + 1) * cols] = turned.astype(BF16)
    shaded = radiosity[...].reshape(bands * leaves, leaf).astype(BF16)
    copies[1].wait()
    leaf_twice = own_blocks(dot(shaded, basis[...], NT), leaves)
    leaf_coef = leaf_twice[:, :RANK].astype(BF16)
    copies[2].wait()
    parts = jnp.zeros((bands * leaves, RANK), F32)
    which = row_of(parts.shape, leaves)
    for at in range(leaves):
        parts += jnp.where(which == at, dot(leaf_coef, up_leaf[at], NN), 0.0)
    pair = jnp.sum(parts.reshape(bands, rows, cols, RANK), axis=1).reshape(bands * cols, RANK)
    pair_coef = pair.astype(BF16)
    copies[3].wait()
    parts = jnp.zeros((bands * cols, RANK), F32)
    which = row_of(parts.shape, cols)
    for at in range(cols):
        parts += jnp.where(which == at, dot(pair_coef, up_pair[at], NN), 0.0)
    top = jnp.sum(parts.reshape(bands, cols, RANK), axis=1)
    top_twice = jnp.concatenate([top, top], axis=1)
    pair_twice = jnp.concatenate([pair, pair], axis=1)

    def edge(col):
        return jnp.concatenate(
            [radiosity[:, g, col, :] for g in range(rows)], axis=1
        )

    leaf_part = side_by_side(leaf_twice, leaves)
    pair_part = side_by_side(pair_twice, cols)
    top_part = jnp.concatenate([top_twice, jnp.zeros_like(top_twice)], axis=0)

    def block(col):
        return jnp.concatenate(
            [leaf_part, jnp.concatenate([pair_part, edge(col)], axis=0), top_part], axis=1
        ).astype(BF16)

    first = block(0)
    for to in range(sent.shape[0]):
        sent[to] = first
    sent[(column + 1) % sent.shape[0]] = block(cols - 1)


def packing_kernel(place, ring, cells, packed, tops):
    column = place[1]
    around, leaves = ring.shape[:2]
    cols = leaves // 2
    for at in range(around):
        packed[at * leaves : (at + 1) * leaves] = ring[at, :, :512]
        tops[:, at] = jnp.broadcast_to(ring[at, :, 1024:][None, :8], (tops.shape[0], 8, LANES))
    for at in range(0, around, 2):
        start = around * leaves + at * cols
        both = [ring[at + k, :, 512:1024].astype(F32)[:cols] for k in range(2)]
        packed[start : start + 2 * cols] = jnp.concatenate(both, axis=0).astype(BF16)
    start = around * (leaves + cols)
    for at in range(0, leaves, 4):
        four = [cells[at + k].astype(F32) for k in range(4)]
        two = [jnp.concatenate(four[:2], axis=1), jnp.concatenate(four[2:], axis=1)]
        packed[start + at * 4 : start + at * 4 + 16] = jnp.concatenate(two, axis=0).astype(BF16)
    start += leaves * 4
    sides = [(column + around - 1) % around, (column + 1) % around]
    both = [ring[at, :, 512:1024].astype(F32)[8:] for at in sides]
    packed[start : start + 16] = jnp.concatenate(both, axis=0).astype(BF16)


def chosen(tables, start, size, tier, inner, count):
    picks = inner.shape[1]
    result = jnp.zeros((count * picks, 512), F32)
    at = lax.broadcasted_iota(jnp.int32, (count, size), 1)
    for number, table in enumerate(tables):
        slots = jnp.where(tier == number, inner, -1)
        choose = jnp.concatenate(
            [(at == slots[:, k : k + 1]).astype(F32) for k in range(picks)], axis=0
        ).astype(BF16)
        result += dot(choose, table[start : start + size], NN)
    low = lax.broadcasted_iota(jnp.int32, (count, LANES), 1) < RANK
    bands = []
    for n in range(4):
        even, odd = [], []
        for k in range(0, picks, 2):
            one = result[k * count : (k + 1) * count, n * LANES : (n + 1) * LANES]
            two = result[(k + 1) * count : (k + 2) * count, n * LANES : (n + 1) * LANES]
            even.append(jnp.where(low, one, pltpu.roll(two, RANK, 1)))
            odd.append(jnp.where(low, pltpu.roll(one, RANK, 1), two))
        bands += [jnp.concatenate(even, axis=1), jnp.concatenate(odd, axis=1)]
    return jnp.concatenate(bands, axis=0).astype(BF16)


def field_kernel(
    place,
    own,
    from_mate,
    from_other,
    tops,
    far_listed,
    far_names_leaf,
    far_names_pair,
    far_names_top,
    far_blocks,
    far_couple_leaf,
    far_couple_pair,
    far_couple_top,
    far_basis,
    far_up_leaf,
    far_up_pair,
    far_emission,
    far_reflect,
    out,
    window,
    listed,
    names_leaf,
    names_pair,
    names_top,
    blocks,
    couple_leaf,
    couple_pair,
    couple_top,
    basis,
    up_leaf,
    up_pair,
    emission,
    reflect,
    gathered,
    sems,
):
    leaves, count = blocks.shape[:2]
    lists = started(
        [
            (far_names_leaf, names_leaf),
            (far_names_pair, names_pair),
            (far_names_top, names_top),
            (far_listed, listed),
        ],
        sems,
    )
    block_copies = started(
        [(far_blocks.at[at], blocks.at[at]) for at in range(leaves)], sems, len(lists)
    )
    couple_copies = started(
        [(far_couple_leaf, couple_leaf), (far_couple_pair, couple_pair)], sems, len(lists) + leaves
    )
    later = started(
        [
            (far_couple_top, couple_top),
            (far_basis, basis),
            (far_up_leaf, up_leaf),
            (far_up_pair, up_pair),
            (far_emission, emission),
            (far_reflect, reflect),
        ],
        sems,
        len(lists) + leaves + 2,
    )
    section, column = place[0], place[1]
    bands, rows, cols, leaf = out.shape
    around = (own.shape[0] - 16 - leaves * 4) // (leaves + cols)
    broad = cols + 2
    width_all = around * cols
    odd = section % 2
    cells_at = around * (leaves + cols)
    sides_at = cells_at + leaves * 4

    def seen_row(source, g, at):
        for p in range(0, cols, 4):
            start = cells_at + (g * cols + p) * 4
            four = source[start : start + 16].astype(F32)
            for k in range(4):
                lanes = slice(k % 2 * leaf, (k % 2 + 1) * leaf)
                window[at * broad + 1 + p + k] = four[k // 2 * 8 : (k // 2 + 1) * 8, lanes]
        two = source[sides_at : sides_at + 16].astype(F32)[:, g * leaf : (g + 1) * leaf]
        window[at * broad] = two[:8]
        window[(at + 1) * broad - 1] = two[8:]

    for g in range(rows):
        seen_row(own, g, g + 1)

    @pl.when(odd == 0)
    def _():
        seen_row(from_other, rows - 1, 0)
        seen_row(from_mate, 0, rows + 1)

    @pl.when(odd == 1)
    def _():
        seen_row(from_mate, rows - 1, 0)
        seen_row(from_other, 0, rows + 1)

    for copy in lists:
        copy.wait()
    mate = section + 1 - 2 * odd
    tables = (own, from_mate, from_other)

    def tier_of(source):
        return jnp.where(source == section, 0, jnp.where(source == mate, 1, 2))

    names = names_leaf[...]
    turn = names % width_all
    height = names // width_all
    leaf_pick = chosen(
        tables,
        0,
        around * leaves,
        tier_of(height // rows),
        turn // cols * leaves + height % rows * cols + turn % cols,
        leaves,
    )
    names = names_pair[...]
    turn = names % width_all
    pair_pick = chosen(
        tables,
        around * leaves,
        around * cols,
        tier_of(names // width_all),
        turn,
        cols,
    )
    picks = names_top.shape[1]
    square = (picks, picks)
    names = jnp.broadcast_to(names_top[...], square)
    diagonal = lax.broadcasted_iota(jnp.int32, square, 0) == lax.broadcasted_iota(jnp.int32, square, 1)
    names = jnp.sum(jnp.where(diagonal, names, 0), axis=1, keepdims=True)
    at = lax.broadcasted_iota(jnp.int32, (picks, tops.shape[0]), 1)
    choose_top = jnp.concatenate(
        [(at == names * bands + b).astype(F32) for b in range(bands)], axis=0
    ).astype(BF16)

    for at in range(leaves):
        seen = []
        for n in range(count):
            name = listed[n, at // cols, at % cols]
            up = name // width_all - rows * section + 1
            turn = (name % width_all + width_all + 1 - cols * column) % width_all
            seen.append(window[up * broad + turn].astype(BF16))
        block_copies[at].wait()
        total = jnp.zeros((bands, leaf), F32)
        turned = jnp.zeros((leaf, bands), F32)
        for n in range(count):
            if n % 2 == 0:
                total += dot(seen[n], blocks[at, n], NT)
            else:
                turned += dot(blocks[at, n], seen[n], NT)
        gathered[at] = total + turned.T
    couple_copies[0].wait()
    leaf_field = own_blocks(dot(leaf_pick, couple_leaf[...], NT), leaves)[:, :RANK]
    couple_copies[1].wait()
    pair_field = own_blocks(dot(pair_pick, couple_pair[...], NT), cols)[:, :RANK]
    for copy in later:
        copy.wait()
    top_pick = dot(choose_top, tops[...], NN)
    top_pick = jnp.concatenate([top_pick] * (picks // 2), axis=1)
    kept = row_of(top_pick.shape, picks) == lax.broadcasted_iota(jnp.int32, top_pick.shape, 1) // RANK
    top_pick = jnp.where(kept, top_pick, 0.0).astype(BF16)
    top_field = dot(top_pick, couple_top[...], NT)
    top_field = jnp.sum(top_field.reshape(bands, picks, RANK), axis=1)
    spread = jnp.broadcast_to(top_field[:, None, :], (bands, cols, RANK))
    spread = spread.reshape(bands * cols, RANK).astype(BF16)
    pair_total = pair_field + own_blocks(dot(spread, up_pair[...], NT), cols)[:, :RANK]
    spread = jnp.broadcast_to(
        pair_total.reshape(bands, 1, cols, RANK), (bands, rows, cols, RANK)
    )
    spread = spread.reshape(bands * leaves, RANK).astype(BF16)
    leaf_total = leaf_field + own_blocks(dot(spread, up_leaf[...], NT), leaves)[:, :RANK]
    leaf_total = leaf_total.astype(BF16)
    far_part = jnp.zeros((bands * leaves, leaf), F32)
    which = row_of(far_part.shape, leaves)
    for at in range(leaves):
        far_part += jnp.where(which == at, dot(leaf_total, basis[at], NN), 0.0)
    far_part = far_part.reshape(out.shape)
    for g in range(rows):
        near_part = jnp.swapaxes(gathered[g * cols : (g + 1) * cols], 0, 1)
        out[:, g] = emission[:, g] + reflect[:, g] * (near_part + far_part[:, g])


def body(
    radiosity,
    emission,
    reflect,
    basis,
    up_leaf,
    upward_pair_transfer,
    near_block,
    couple_leaf,
    couple_pair,
    couple_top,
    near_list,
    far_leaf,
    far_pair,
    far_top,
):
    around = lax.axis_size("perim")
    tall = lax.axis_size("section")
    bands, rows, cols, leaf = radiosity.shape
    leaves = rows * cols
    place = jnp.stack([lax.axis_index("section"), lax.axis_index("perim")]).astype(jnp.int32)
    mates = [(s, s ^ 1) for s in range(tall)]
    others = [(s, s + 1 if s % 2 else s - 1) for s in range(1, tall - 1)]
    sems = pltpu.SemaphoreType.DMA
    basis_wide = far(basis.reshape(leaves * RANK, leaf))
    basis = far(basis.reshape(leaves, RANK, leaf))
    up_leaf_wide = far(up_leaf.reshape(leaves * RANK, RANK))
    up_leaf = far(up_leaf.reshape(leaves, RANK, RANK))
    up_pair_wide = far(upward_pair_transfer.reshape(cols * RANK, RANK))
    up_pair = far(upward_pair_transfer[0])
    sent, cells = pl.pallas_call(
        coefficients_kernel,
        out_shape=[
            jax.ShapeDtypeStruct((around, 16, WIDE), BF16),
            jax.ShapeDtypeStruct((leaves, bands, leaf), BF16),
        ],
        in_specs=[SMEM] + [HBM] * 4,
        out_specs=[VMEM] * 2,
        scratch_shapes=[
            pltpu.VMEM(radiosity.shape, F32),
            pltpu.VMEM(basis_wide.shape, BF16),
            pltpu.VMEM(up_leaf.shape, BF16),
            pltpu.VMEM(up_pair.shape, BF16),
            sems((4,)),
        ],
        compiler_params=limit(12),
        name="coefficients",
    )(place, far(radiosity), basis_wide, up_leaf, up_pair)
    ring = lax.all_to_all(sent, "perim", 0, 0)
    packed, tops = pl.pallas_call(
        packing_kernel,
        out_shape=[
            jax.ShapeDtypeStruct((around * (leaves + cols) + leaves * 4 + 16, 512), BF16),
            jax.ShapeDtypeStruct((tall, around, bands, LANES), BF16),
        ],
        in_specs=[SMEM, VMEM, VMEM],
        out_specs=[VMEM] * 2,
        compiler_params=limit(8),
        name="packing",
    )(place, ring, cells)
    from_mate = lax.ppermute(packed, "section", mates)
    from_other = lax.ppermute(packed, "section", others)
    tops = lax.all_to_all(tops, "section", 0, 0)
    blocks = near_block.reshape((leaves,) + near_block.shape[2:])
    couple_leaf = couple_leaf.reshape(leaves * RANK, -1)
    couple_pair = couple_pair.reshape(cols * RANK, -1)
    couple_top = couple_top[0, 0]
    listed = near_list.transpose(2, 0, 1)
    names_leaf = far_leaf.reshape(leaves, -1)
    names_pair = far_pair.reshape(cols, -1)
    names_top = far_top.reshape(1, -1)
    passed = [couple_top, basis, up_leaf_wide, up_pair_wide, emission, reflect]
    held = [names_leaf, names_pair, names_top, blocks, couple_leaf, couple_pair] + passed
    return pl.pallas_call(
        field_kernel,
        out_shape=jax.ShapeDtypeStruct(radiosity.shape, F32),
        in_specs=[SMEM] + [VMEM] * 4 + [HBM] * 13,
        out_specs=VMEM,
        scratch_shapes=[
            pltpu.VMEM(((rows + 2) * (cols + 2), bands, leaf), F32),
            pltpu.SMEM(listed.shape, jnp.int32),
        ]
        + [pltpu.VMEM(x.shape, x.dtype) for x in held]
        + [pltpu.VMEM((leaves, bands, leaf), F32), sems((leaves + 12,))],
        compiler_params=limit(32),
        name="fields",
    )(
        place,
        packed,
        from_mate,
        from_other,
        tops.reshape(tall * around * bands, LANES),
        far(listed),
        *map(far, held),
    )


def solution(mesh):
    cells = P(None, "section", "perim", None)
    four = P("section", "perim", None, None)
    lists = P("section", "perim", None)
    return jax.shard_map(
        body,
        mesh=mesh,
        in_specs=(cells,) * 3
        + (four,) * 3
        + (P("section", "perim", None, None, None),)
        + (four,) * 3
        + (lists,) * 4,
        out_specs=cells,
        check_vma=False,
    )
```

```python
import jax
import jax.numpy as jnp
from jax import lax
from jax.experimental import pallas as pl
from jax.experimental.pallas import tpu as pltpu
from jax.sharding import PartitionSpec as P

F32 = jnp.float32
BF16 = jnp.bfloat16
NT = (((1,), (1,)), ((), ()))
NN = (((1,), (0,)), ((), ()))
LANES = 128
RANK = 64
WIDE = 1152
VMEM = pl.BlockSpec(memory_space=pltpu.VMEM)
SMEM = pl.BlockSpec(memory_space=pltpu.SMEM)
HBM = pl.BlockSpec(memory_space=pltpu.HBM)
ANY = pl.BlockSpec(memory_space=pl.ANY)
AT_ONCE = 8


def dot(left, right, dims):
    return lax.dot_general(left, right, dims, preferred_element_type=F32)


def far(x):
    return pltpu.with_memory_space_constraint(x, pltpu.HBM)


def limit(mib):
    return pltpu.CompilerParams(vmem_limit_bytes=mib * 1024 * 1024)


def row_of(shape, count):
    return lax.broadcasted_iota(jnp.int32, shape, 0) % count


def own_blocks(products, count):
    shape = (products.shape[0], LANES)
    mine = row_of(shape, count) - lax.broadcasted_iota(jnp.int32, shape, 1) // RANK
    total = jnp.zeros(shape, F32)
    for tile in range(count // 2):
        total += jnp.where(mine == 2 * tile, products[:, tile * LANES : (tile + 1) * LANES], 0.0)
    return total + pltpu.roll(total, RANK, 1)


def side_by_side(twice, count):
    low = lax.broadcasted_iota(jnp.int32, (count, LANES), 1) < RANK
    return jnp.concatenate(
        [
            jnp.where(low, twice[b * count : (b + 1) * count], twice[(b + 1) * count : (b + 2) * count])
            for b in range(0, twice.shape[0] // count, 2)
        ],
        axis=1,
    )


def started(copies, sems, at=0):
    made = []
    for number, (source, target) in enumerate(copies):
        made.append(pltpu.make_async_copy(source, target, sems.at[at + number]))
        made[-1].start()
    return made


def coefficients_kernel(
    place,
    far_radiosity,
    far_basis,
    far_up_leaf,
    far_up_pair,
    sent,
    cells,
    radiosity,
    basis,
    up_leaf,
    up_pair,
    block,
    sems,
):
    copies = started(
        [
            (far_radiosity, radiosity),
            (far_basis, basis),
            (far_up_leaf, up_leaf),
            (far_up_pair, up_pair),
        ],
        sems,
    )
    copies[0].wait()
    column = place[1]
    bands, rows, cols, leaf = radiosity.shape
    leaves = rows * cols
    for g in range(rows):
        turned = jnp.swapaxes(radiosity[:, g], 0, 1)
        cells[g * cols : (g + 1) * cols] = turned.astype(BF16)
    shaded = radiosity[...].reshape(bands * leaves, leaf).astype(BF16)
    copies[1].wait()
    leaf_twice = own_blocks(dot(shaded, basis[...], NT), leaves)
    leaf_coef = leaf_twice[:, :RANK].astype(BF16)
    copies[2].wait()
    parts = jnp.zeros((bands * leaves, RANK), F32)
    which = row_of(parts.shape, leaves)
    for at in range(leaves):
        parts += jnp.where(which == at, dot(leaf_coef, up_leaf[at], NN), 0.0)
    pair = jnp.sum(parts.reshape(bands, rows, cols, RANK), axis=1).reshape(bands * cols, RANK)
    pair_coef = pair.astype(BF16)
    copies[3].wait()
    parts = jnp.zeros((bands * cols, RANK), F32)
    which = row_of(parts.shape, cols)
    for at in range(cols):
        parts += jnp.where(which == at, dot(pair_coef, up_pair[at], NN), 0.0)
    top = jnp.sum(parts.reshape(bands, cols, RANK), axis=1)
    top_twice = jnp.concatenate([top, top], axis=1)
    pair_twice = jnp.concatenate([pair, pair], axis=1)

    def edge(col):
        return jnp.concatenate(
            [radiosity[:, g, col, :] for g in range(rows)], axis=1
        )

    leaf_part = side_by_side(leaf_twice, leaves)
    pair_part = side_by_side(pair_twice, cols)
    top_part = jnp.concatenate([top_twice, jnp.zeros_like(top_twice)], axis=0)

    for right, col in enumerate((0, cols - 1)):
        block[right] = jnp.concatenate(
            [leaf_part, jnp.concatenate([pair_part, edge(col)], axis=0), top_part], axis=1
        ).astype(BF16)
    around = sent.shape[0]
    to_right = (column + 1) % around
    copies = started(
        [(block.at[jnp.where(to_right == to, 1, 0)], sent.at[to]) for to in range(around)], sems, 4
    )
    for copy in copies:
        copy.wait()


def packing_kernel(place, ring, cells, local_part, packed):
    column = place[1]
    around, leaves = ring.shape[:2]
    cols = leaves // 2
    for at in range(around):
        packed[at * leaves : (at + 1) * leaves] = ring[at, :, :512]
    for at in range(0, around, 2):
        start = around * leaves + at * cols
        both = [ring[at + k, :, 512:1024].astype(F32)[:cols] for k in range(2)]
        packed[start : start + 2 * cols] = jnp.concatenate(both, axis=0).astype(BF16)
    start = around * (leaves + cols)
    for at in range(0, leaves, 4):
        four = [cells[at + k].astype(F32) for k in range(4)]
        two = [jnp.concatenate(four[:2], axis=1), jnp.concatenate(four[2:], axis=1)]
        packed[start + at * 4 : start + at * 4 + 16] = jnp.concatenate(two, axis=0).astype(BF16)
    start += leaves * 4
    sides = [(column + around - 1) % around, (column + 1) % around]
    both = [ring[at, :, 512:1024].astype(F32)[8:] for at in sides]
    packed[start : start + 16] = jnp.concatenate(both, axis=0).astype(BF16)


def tops_kernel(ring, tops, row_tops, sems):
    row_tops[...] = ring[:, :8, 1024:]
    for copy in started([(row_tops, tops.at[to]) for to in range(tops.shape[0])], sems):
        copy.wait()


def one_hot(tier, inner, size):
    count, picks = inner.shape
    slots = tier * size + inner
    at = lax.broadcasted_iota(jnp.int32, (count, 3 * size), 1)
    return jnp.concatenate(
        [(at == slots[:, k : k + 1]).astype(F32) for k in range(picks)], axis=0
    ).astype(BF16)


def near_products(seen, blocks):
    total = jnp.zeros(seen[0].shape, F32)
    turned = jnp.zeros(seen[0].shape[::-1], F32)
    for n, cell in enumerate(seen):
        if n % 2 == 0:
            total += dot(cell, blocks[n], NT)
        else:
            turned += dot(blocks[n], cell, NT)
    return total + turned.T


def split_name(name, width_all):
    if width_all & (width_all - 1):
        return name // width_all, name % width_all
    return name >> (width_all.bit_length() - 1), name & (width_all - 1)


def position(name, section, column, rows, cols, width_all):
    row = split_name(name, width_all)[0]
    turn = split_name(name + (width_all + 1 - cols * column), width_all)[1]
    return row - (rows * section - 1), turn


def local_kernel(
    place,
    cells,
    far_listed,
    far_names_leaf,
    far_names_pair,
    far_names_top,
    far_blocks,
    far_choose_leaf,
    far_choose_pair,
    far_choose_top,
    far_local_part,
    far_todo,
    window,
    listed,
    todo,
    names_leaf,
    names_pair,
    names_top,
    blocks,
    choose_leaf,
    choose_pair,
    choose_top,
    local_part,
    sems,
):
    leaves, count = blocks.shape[:2]
    lists = started(
        [
            (far_names_leaf, names_leaf),
            (far_names_pair, names_pair),
            (far_names_top, names_top),
            (far_listed, listed),
        ],
        sems,
    )
    block_copies = started(
        [(far_blocks.at[at], blocks.at[at]) for at in range(leaves)], sems, len(lists)
    )
    for copy in lists:
        copy.wait()
    section = place[0]
    cols = names_pair.shape[0]
    rows = leaves // cols
    width_all = choose_pair.shape[1] // 3
    mate = section + 1 - 2 * (section % 2)

    def tier_of(source):
        return jnp.where(source == section, 0, jnp.where(source == mate, 1, 2))

    names = names_leaf[...]
    height, turn = split_name(names, width_all)
    source, height = split_name(height, rows)
    device, turn = split_name(turn, cols)
    choose_leaf[...] = one_hot(
        tier_of(source), device * leaves + height * cols + turn, width_all * rows
    )
    height, turn = split_name(names_pair[...], width_all)
    choose_pair[...] = one_hot(tier_of(height), turn, width_all)
    picks = names_top.shape[1]
    bands = choose_top.shape[0] // picks
    square = (picks, picks)
    names = jnp.broadcast_to(names_top[...], square)
    diagonal = lax.broadcasted_iota(jnp.int32, square, 0) == lax.broadcasted_iota(jnp.int32, square, 1)
    names = jnp.sum(jnp.where(diagonal, names, 0), axis=1, keepdims=True)
    at = lax.broadcasted_iota(jnp.int32, (picks, choose_top.shape[1]), 1)
    choose_top[...] = jnp.concatenate(
        [(at == names * bands + b).astype(F32) for b in range(bands)], axis=0
    ).astype(BF16)
    results = started(
        [
            (choose_leaf, far_choose_leaf),
            (choose_pair, far_choose_pair),
            (choose_top, far_choose_top),
        ],
        sems,
        len(lists) + leaves,
    )
    broad = cols + 2
    window[...] = jnp.zeros_like(window)
    for g in range(rows):
        start = (g + 1) * broad + 1
        window[start : start + cols] = cells[g * cols : (g + 1) * cols].astype(F32)
    found = jnp.int32(0)
    for at in range(leaves):
        seen = []
        for n in range(count):
            name = listed[n, at // cols, at % cols]
            up, turn = position(name, section, place[1], rows, cols, width_all)
            where = up * broad + turn
            seen.append(window[where].astype(BF16))
            if n > 0:
                todo[0, found] = (where << 12) + (at << 4) + n
                inside = (up >= 1) & (up <= rows) & (turn >= 1) & (turn <= cols)
                found = found + jnp.where(inside, 0, 1)
        if at % 2 == 0:
            for copy in block_copies[at : at + 2]:
                copy.wait()
        local_part[at] = near_products(seen, blocks.at[at])
    todo[0, todo.shape[1] - 1] = found
    results += started(
        [(local_part, far_local_part), (todo, far_todo)], sems, len(lists) + leaves + 3
    )
    for copy in results:
        copy.wait()


def chosen(choose, tables, start, count):
    size = choose.shape[1] // 3
    picks = choose.shape[0] // count
    result = jnp.zeros((count * picks, 512), F32)
    for number, table in enumerate(tables):
        result += dot(
            choose[:, number * size : (number + 1) * size], table[start : start + size], NN
        )
    low = lax.broadcasted_iota(jnp.int32, (count, LANES), 1) < RANK
    bands = []
    for n in range(4):
        even, odd = [], []
        for k in range(0, picks, 2):
            one = result[k * count : (k + 1) * count, n * LANES : (n + 1) * LANES]
            two = result[(k + 1) * count : (k + 2) * count, n * LANES : (n + 1) * LANES]
            even.append(jnp.where(low, one, pltpu.roll(two, RANK, 1)))
            odd.append(jnp.where(low, pltpu.roll(one, RANK, 1), two))
        bands += [jnp.concatenate(even, axis=1), jnp.concatenate(odd, axis=1)]
    return jnp.concatenate(bands, axis=0).astype(BF16)


def field_kernel(
    place,
    own,
    from_mate,
    from_other,
    far_todo,
    far_choose_leaf,
    far_choose_pair,
    far_choose_top,
    far_gathered,
    far_emission,
    far_reflect,
    far_couple_leaf,
    far_couple_pair,
    far_blocks,
    parts,
    fields,
    choose_top,
    window,
    todo,
    choose_leaf,
    choose_pair,
    gathered,
    emission,
    reflect,
    couple_leaf,
    couple_pair,
    blocks,
    sems,
    block_sems,
):
    copies = started(
        [
            (far_todo, todo),
            (far_choose_leaf, choose_leaf),
            (far_choose_pair, choose_pair),
            (far_couple_leaf, couple_leaf),
            (far_couple_pair, couple_pair),
            (far_gathered, gathered),
            (far_choose_top, choose_top),
            (far_emission, emission),
            (far_reflect, reflect),
        ],
        sems,
    )
    leaves = gathered.shape[0]
    section, column = place[0], place[1]
    bands, rows, cols, leaf = emission.shape
    around = (own.shape[0] - 16 - leaves * 4) // (leaves + cols)
    broad = cols + 2
    width_all = around * cols
    odd = section % 2
    cells_at = around * (leaves + cols)
    sides_at = cells_at + leaves * 4

    def seen_row(source, g, at):
        for p in range(0, cols, 4):
            start = cells_at + (g * cols + p) * 4
            four = source[start : start + 16].astype(F32)
            for k in range(4):
                lanes = slice(k % 2 * leaf, (k % 2 + 1) * leaf)
                window[at * broad + 1 + p + k] = four[k // 2 * 8 : (k // 2 + 1) * 8, lanes]
        two = source[sides_at : sides_at + 16].astype(F32)[:, g * leaf : (g + 1) * leaf]
        window[at * broad] = two[:8]
        window[(at + 1) * broad - 1] = two[8:]

    for g in range(rows):
        seen_row(own, g, g + 1)

    @pl.when(odd == 0)
    def _():
        seen_row(from_other, rows - 1, 0)
        seen_row(from_mate, 0, rows + 1)

    @pl.when(odd == 1)
    def _():
        seen_row(from_mate, rows - 1, 0)
        seen_row(from_other, 0, rows + 1)

    zero_cell = window.shape[0] - 1
    window[zero_cell] = jnp.zeros(window.shape[1:], F32)
    copies[0].wait()

    found = todo[0, todo.shape[1] - 1]

    def block_copy(at, n, slot):
        return pltpu.make_async_copy(
            far_blocks.at[at, n], blocks.at[slot], block_sems.at[slot]
        )

    def fetch(slot, _):
        pair = todo[0, slot]
        block_copy((pair >> 4) & 255, pair & 15, slot).start()
        return 0

    lax.fori_loop(0, found, fetch, 0)
    tables = (own, from_mate, from_other)
    copies[1].wait()
    leaf_pick = chosen(choose_leaf, tables, 0, leaves)
    copies[2].wait()
    pair_pick = chosen(choose_pair, tables, around * leaves, cols)
    split = bands * leaves
    copies[3].wait()
    fields[:split] = own_blocks(dot(leaf_pick, couple_leaf[...], NT), leaves)
    copies[4].wait()
    fields[split:] = own_blocks(dot(pair_pick, couple_pair[...], NT), cols)
    for copy in copies[5:]:
        copy.wait()

    def several(step, _):
        first = step * AT_ONCE
        for k in range(AT_ONCE):

            @pl.when(first + k < found)
            def _():
                block_copy(0, 0, first + k).wait()

        results = []
        for k in range(AT_ONCE):
            slot = jnp.minimum(first + k, found - 1)
            where = jnp.where(first + k < found, todo[0, slot] >> 12, zero_cell)
            cell = window[where].astype(BF16)
            if k % 2 == 0:
                results.append(dot(cell, blocks[slot], NT))
            else:
                results.append(dot(blocks[slot], cell, NT).T)
        for k in range(AT_ONCE):
            at = (todo[0, jnp.minimum(first + k, found - 1)] >> 4) & 255
            gathered[at] += results[k]
        return 0

    lax.fori_loop(0, (found + AT_ONCE - 1) // AT_ONCE, several, 0)
    for g in range(rows):
        near_part = jnp.swapaxes(gathered[g * cols : (g + 1) * cols], 0, 1)
        parts[0, :, g] = emission[:, g] + reflect[:, g] * near_part
        parts[1, :, g] = reflect[:, g]


def result_kernel(tops, parts, fields, choose_top, couple_top, basis, up_leaf, up_pair, out):
    bands, rows, cols, leaf = out.shape
    leaves = rows * cols
    picks = couple_top.shape[1] // RANK
    leaf_field = fields[: bands * leaves, :RANK]
    pair_field = fields[bands * leaves :, :RANK]
    top_pick = dot(choose_top[...], tops[...], NN)
    top_pick = jnp.concatenate([top_pick] * (picks // 2), axis=1)
    kept = row_of(top_pick.shape, picks) == lax.broadcasted_iota(jnp.int32, top_pick.shape, 1) // RANK
    top_pick = jnp.where(kept, top_pick, 0.0).astype(BF16)
    top_field = dot(top_pick, couple_top[...], NT)
    top_field = jnp.sum(top_field.reshape(bands, picks, RANK), axis=1)
    spread = jnp.broadcast_to(top_field[:, None, :], (bands, cols, RANK))
    spread = spread.reshape(bands * cols, RANK).astype(BF16)
    pair_total = pair_field + own_blocks(dot(spread, up_pair[...], NT), cols)[:, :RANK]
    spread = jnp.broadcast_to(
        pair_total.reshape(bands, 1, cols, RANK), (bands, rows, cols, RANK)
    )
    spread = spread.reshape(bands * leaves, RANK).astype(BF16)
    leaf_total = leaf_field + own_blocks(dot(spread, up_leaf[...], NT), leaves)[:, :RANK]
    leaf_total = leaf_total.astype(BF16)
    far_part = jnp.zeros((bands * leaves, leaf), F32)
    which = row_of(far_part.shape, leaves)
    for at in range(leaves):
        far_part += jnp.where(which == at, dot(leaf_total, basis[at], NN), 0.0)
    out[...] = parts[0] + parts[1] * far_part.reshape(out.shape)


def body(
    radiosity,
    emission,
    reflect,
    basis,
    up_leaf,
    upward_pair_transfer,
    near_block,
    couple_leaf,
    couple_pair,
    couple_top,
    near_list,
    far_leaf,
    far_pair,
    far_top,
):
    around = lax.axis_size("perim")
    tall = lax.axis_size("section")
    bands, rows, cols, leaf = radiosity.shape
    leaves = rows * cols
    place = jnp.stack([lax.axis_index("section"), lax.axis_index("perim")]).astype(jnp.int32)
    mates = [(s, s ^ 1) for s in range(tall)]
    others = [(s, s + 1 if s % 2 else s - 1) for s in range(1, tall - 1)]
    sems = pltpu.SemaphoreType.DMA
    basis_wide = basis.reshape(leaves * RANK, leaf)
    basis = basis.reshape(leaves, RANK, leaf)
    up_leaf_wide = up_leaf.reshape(leaves * RANK, RANK)
    up_leaf = up_leaf.reshape(leaves, RANK, RANK)
    up_pair_wide = upward_pair_transfer.reshape(cols * RANK, RANK)
    up_pair = upward_pair_transfer[0]
    sent, cells = pl.pallas_call(
        coefficients_kernel,
        out_shape=[
            pltpu.HBM((around, 16, WIDE), BF16),
            jax.ShapeDtypeStruct((leaves, bands, leaf), BF16),
        ],
        in_specs=[SMEM] + [HBM] * 4,
        out_specs=[HBM, VMEM],
        scratch_shapes=[
            pltpu.VMEM(radiosity.shape, F32),
            pltpu.VMEM(basis_wide.shape, BF16),
            pltpu.VMEM(up_leaf.shape, BF16),
            pltpu.VMEM(up_pair.shape, BF16),
            pltpu.VMEM((2, 16, WIDE), BF16),
            sems((around + 4,)),
        ],
        compiler_params=limit(12),
        name="coefficients",
    )(place, *map(far, [radiosity, basis_wide, up_leaf, up_pair]))
    ring = lax.all_to_all(sent, "perim", 0, 0)
    blocks = near_block.reshape((leaves,) + near_block.shape[2:])
    couple_leaf = couple_leaf.reshape(leaves * RANK, -1)
    couple_pair = couple_pair.reshape(cols * RANK, -1)
    couple_top = couple_top[0, 0]
    listed = near_list.transpose(2, 0, 1)
    names_leaf = far_leaf.reshape(leaves, -1)
    names_pair = far_pair.reshape(cols, -1)
    names_top = far_top.reshape(1, -1)
    names = [names_leaf, names_pair, names_top]
    window = ((rows + 2) * (cols + 2), bands, leaf)
    choices = [
        pltpu.HBM((names_leaf.size, 3 * around * leaves), BF16),
        pltpu.HBM((names_pair.size, 3 * around * cols), BF16),
        pltpu.HBM((bands * names_top.size, tall * around * bands), BF16),
        pltpu.HBM((leaves, bands, leaf), F32),
        pltpu.HBM((1, LANES), jnp.int32),
    ]
    choose_leaf, choose_pair, choose_top, local_part, todo = pl.pallas_call(
        local_kernel,
        out_shape=choices,
        in_specs=[SMEM, VMEM] + [HBM] * 5,
        out_specs=[HBM] * 5,
        scratch_shapes=[
            pltpu.VMEM(window, F32),
            pltpu.SMEM(listed.shape, jnp.int32),
            pltpu.SMEM((1, LANES), jnp.int32),
        ]
        + [pltpu.VMEM(x.shape, x.dtype) for x in names + [blocks] + choices[:4]]
        + [sems((leaves + 9,))],
        compiler_params=limit(28),
        name="local",
    )(place, cells, *map(far, [listed] + names + [blocks]))
    packed = pl.pallas_call(
        packing_kernel,
        out_shape=jax.ShapeDtypeStruct((around * (leaves + cols) + leaves * 4 + 16, 512), BF16),
        in_specs=[SMEM, VMEM, VMEM, HBM],
        out_specs=VMEM,
        compiler_params=limit(8),
        name="packing",
    )(place, ring, cells, far(local_part))
    tops = pl.pallas_call(
        tops_kernel,
        out_shape=pltpu.HBM((tall, around, bands, LANES), BF16),
        in_specs=[VMEM],
        out_specs=HBM,
        scratch_shapes=[pltpu.VMEM((around, bands, LANES), BF16), sems((tall,))],
        compiler_params=limit(8),
        name="tops",
    )(ring)
    from_mate = lax.ppermute(packed, "section", mates)
    from_other = lax.ppermute(packed, "section", others)
    tops = lax.all_to_all(tops, "section", 0, 0)
    most = leaves * (listed.shape[0] - 1)
    held = [choose_leaf, choose_pair, local_part, emission, reflect, couple_leaf, couple_pair]
    parts, fields, choose_top = pl.pallas_call(
        field_kernel,
        out_shape=[
            jax.ShapeDtypeStruct((2,) + radiosity.shape, F32),
            jax.ShapeDtypeStruct((bands * (leaves + cols), LANES), F32),
            jax.ShapeDtypeStruct(choose_top.shape, BF16),
        ],
        in_specs=[SMEM] + [VMEM] * 3 + [HBM] * 10,
        out_specs=[VMEM] * 3,
        scratch_shapes=[
            pltpu.VMEM((window[0] + 1,) + window[1:], F32),
            pltpu.SMEM(todo.shape, jnp.int32),
        ]
        + [pltpu.VMEM(x.shape, x.dtype) for x in held]
        + [pltpu.VMEM((most, leaf, leaf), BF16), sems((9,)), sems((most,))],
        compiler_params=limit(28),
        name="fields",
    )(
        place,
        packed,
        from_mate,
        from_other,
        *map(far, [todo] + held[:2] + [choose_top] + held[2:] + [blocks]),
    )
    return pl.pallas_call(
        result_kernel,
        out_shape=jax.ShapeDtypeStruct(radiosity.shape, F32),
        in_specs=[VMEM] * 8,
        out_specs=VMEM,
        compiler_params=limit(8),
        name="result",
    )(
        tops.reshape(tall * around * bands, LANES),
        parts,
        fields,
        choose_top,
        couple_top,
        basis,
        up_leaf_wide,
        up_pair_wide,
    )


def solution(mesh):
    cells = P(None, "section", "perim", None)
    four = P("section", "perim", None, None)
    lists = P("section", "perim", None)
    return jax.shard_map(
        body,
        mesh=mesh,
        in_specs=(cells,) * 3
        + (four,) * 3
        + (P("section", "perim", None, None, None),)
        + (four,) * 3
        + (lists,) * 4,
        out_specs=cells,
        check_vma=False,
    )
```

```python
import jax
import jax.numpy as jnp
from jax import lax
from jax.experimental import pallas as pl
from jax.experimental.pallas import tpu as pltpu
from jax.sharding import PartitionSpec as P

F32 = jnp.float32
BF16 = jnp.bfloat16
NT = (((1,), (1,)), ((), ()))
NN = (((1,), (0,)), ((), ()))
LANES = 128
RANK = 64
WIDE = 1152
VMEM = pl.BlockSpec(memory_space=pltpu.VMEM)
HBM = pl.BlockSpec(memory_space=pltpu.HBM)
ANY = pl.BlockSpec(memory_space=pl.ANY)
AT_ONCE = 16


def dot(left, right, dims):
    return lax.dot_general(left, right, dims, preferred_element_type=F32)


def far(x):
    return pltpu.with_memory_space_constraint(x, pltpu.HBM)


def limit(mib):
    return pltpu.CompilerParams(vmem_limit_bytes=mib * 1024 * 1024)


def row_of(shape, count):
    return lax.broadcasted_iota(jnp.int32, shape, 0) % count


def own_blocks(products, count):
    shape = (products.shape[0], LANES)
    mine = row_of(shape, count) - lax.broadcasted_iota(jnp.int32, shape, 1) // RANK
    total = jnp.zeros(shape, F32)
    for tile in range(count // 2):
        total += jnp.where(mine == 2 * tile, products[:, tile * LANES : (tile + 1) * LANES], 0.0)
    return total + pltpu.roll(total, RANK, 1)


def on_diagonal(twice, count):
    mine = row_of(twice.shape, count) - lax.broadcasted_iota(jnp.int32, twice.shape, 1) // RANK
    tiles = [jnp.where(mine == 2 * tile, twice, 0.0) for tile in range(count // 2)]
    return jnp.concatenate(tiles, axis=1).astype(BF16)


def side_by_side(twice, count):
    low = lax.broadcasted_iota(jnp.int32, (count, LANES), 1) < RANK
    return jnp.concatenate(
        [
            jnp.where(low, twice[b * count : (b + 1) * count], twice[(b + 1) * count : (b + 2) * count])
            for b in range(0, twice.shape[0] // count, 2)
        ],
        axis=1,
    )


def started(copies, sems, at=0):
    made = []
    for number, (source, target) in enumerate(copies):
        made.append(pltpu.make_async_copy(source, target, sems.at[at + number]))
        made[-1].start()
    return made


def coefficients_kernel(
    far_radiosity,
    far_basis,
    far_up_leaf,
    far_up_pair,
    sent,
    cells,
    radiosity,
    basis,
    up_leaf,
    up_pair,
    block,
    sems,
):
    copies = started(
        [
            (far_radiosity, radiosity),
            (far_basis, basis),
            (far_up_leaf, up_leaf),
            (far_up_pair, up_pair),
        ],
        sems,
    )
    copies[0].wait()
    column = lax.axis_index("perim")
    bands, rows, cols, leaf = radiosity.shape
    leaves = rows * cols
    shaded = radiosity[...].reshape(bands * leaves, leaf).astype(BF16)
    copies[1].wait()
    leaf_twice = own_blocks(dot(shaded, basis[...], NT), leaves)
    of_pairs = leaf_twice.reshape(bands, rows, cols, LANES)
    of_pairs = jnp.concatenate(
        [on_diagonal(of_pairs[:, g].reshape(bands * cols, LANES), cols) for g in range(rows)],
        axis=1,
    )
    copies[2].wait()
    pair = dot(of_pairs, up_leaf[...], NN)
    pair_twice = jnp.concatenate([pair, pair], axis=1)
    copies[3].wait()
    top = dot(on_diagonal(pair_twice, cols), up_pair[...], NN)
    top = jnp.sum(top.reshape(bands, cols, RANK), axis=1)
    top_twice = jnp.concatenate([top, top], axis=1)

    def edge(col):
        return jnp.concatenate(
            [radiosity[:, g, col, :] for g in range(rows)], axis=1
        )

    leaf_part = side_by_side(leaf_twice, leaves)
    pair_part = side_by_side(pair_twice, cols)
    top_part = jnp.concatenate([top_twice, jnp.zeros_like(top_twice)], axis=0)

    for right, col in enumerate((0, cols - 1)):
        block[right] = jnp.concatenate(
            [leaf_part, jnp.concatenate([pair_part, edge(col)], axis=0), top_part], axis=1
        ).astype(BF16)
    around = sent.shape[0]
    to_right = (column + 1) % around
    copies = started(
        [(block.at[jnp.where(to_right == to, 1, 0)], sent.at[to]) for to in range(around)], sems, 4
    )
    for g in range(rows):
        turned = jnp.swapaxes(radiosity[:, g], 0, 1)
        cells[g * cols : (g + 1) * cols] = turned.astype(BF16)
    for copy in copies:
        copy.wait()


def packing_kernel(ring, cells, local_part, packed):
    column = lax.axis_index("perim")
    around, leaves = ring.shape[:2]
    cols = leaves // 2
    for at in range(around):
        packed[at * leaves : (at + 1) * leaves] = ring[at, :, :512]
    for at in range(0, around, 2):
        start = around * leaves + at * cols
        both = [ring[at + k, :, 512:1024].astype(F32)[:cols] for k in range(2)]
        packed[start : start + 2 * cols] = jnp.concatenate(both, axis=0).astype(BF16)
    start = around * (leaves + cols)
    for at in range(0, leaves, 4):
        four = [cells[at + k].astype(F32) for k in range(4)]
        two = [jnp.concatenate(four[:2], axis=1), jnp.concatenate(four[2:], axis=1)]
        packed[start + at * 4 : start + at * 4 + 16] = jnp.concatenate(two, axis=0).astype(BF16)
    start += leaves * 4
    sides = [(column + around - 1) % around, (column + 1) % around]
    both = [ring[at, :, 512:1024].astype(F32)[8:] for at in sides]
    packed[start : start + 16] = jnp.concatenate(both, axis=0).astype(BF16)


def tops_kernel(ring, tops, row_tops, sems):
    row_tops[...] = ring[:, :8, 1024:]
    for copy in started([(row_tops, tops.at[to]) for to in range(tops.shape[0])], sems):
        copy.wait()


def one_hot(tier, inner, size):
    count, picks = inner.shape
    slots = tier * size + inner
    at = lax.broadcasted_iota(jnp.int32, (count, 3 * size), 1)
    return jnp.concatenate(
        [(at == slots[:, k : k + 1]).astype(F32) for k in range(picks)], axis=0
    ).astype(BF16)


def near_products(seen, blocks):
    total = jnp.zeros(seen[0].shape, F32)
    turned = jnp.zeros(seen[0].shape[::-1], F32)
    for n, cell in enumerate(seen):
        if n % 2 == 0:
            total += dot(cell, blocks[n], NT)
        else:
            turned += dot(blocks[n], cell, NT)
    return total + turned.T


def split_name(name, width_all):
    if width_all & (width_all - 1):
        return name // width_all, name % width_all
    return name >> (width_all.bit_length() - 1), name & (width_all - 1)


def position(name, section, column, rows, cols, width_all):
    row = split_name(name, width_all)[0]
    turn = split_name(name + (width_all + 1 - cols * column), width_all)[1]
    return row - (rows * section - 1), turn


def local_kernel(
    cells,
    far_listed,
    far_names_leaf,
    far_names_pair,
    far_names_top,
    far_blocks,
    far_choose_leaf,
    far_choose_pair,
    far_choose_top,
    far_todo,
    local_part,
    window,
    listed,
    todo,
    names_leaf,
    names_pair,
    names_top,
    blocks,
    choose_leaf,
    choose_pair,
    choose_top,
    sems,
):
    leaves, count = blocks.shape[:2]
    lists = started(
        [
            (far_names_leaf, names_leaf),
            (far_names_pair, names_pair),
            (far_names_top, names_top),
            (far_listed, listed),
        ],
        sems,
    )
    block_copies = started(
        [(far_blocks.at[at], blocks.at[at]) for at in range(leaves)], sems, len(lists)
    )
    for copy in lists:
        copy.wait()
    section, column = lax.axis_index("section"), lax.axis_index("perim")
    cols = names_pair.shape[0]
    rows = leaves // cols
    width_all = choose_pair.shape[1] // 3
    mate = section + 1 - 2 * (section % 2)

    def tier_of(source):
        return jnp.where(source == section, 0, jnp.where(source == mate, 1, 2))

    names = names_leaf[...]
    height, turn = split_name(names, width_all)
    source, height = split_name(height, rows)
    device, turn = split_name(turn, cols)
    choose_leaf[...] = one_hot(
        tier_of(source), device * leaves + height * cols + turn, width_all * rows
    )
    height, turn = split_name(names_pair[...], width_all)
    choose_pair[...] = one_hot(tier_of(height), turn, width_all)
    picks = names_top.shape[1]
    bands = choose_top.shape[0] // picks
    square = (picks, picks)
    names = jnp.broadcast_to(names_top[...], square)
    diagonal = lax.broadcasted_iota(jnp.int32, square, 0) == lax.broadcasted_iota(jnp.int32, square, 1)
    names = jnp.sum(jnp.where(diagonal, names, 0), axis=1, keepdims=True)
    at = lax.broadcasted_iota(jnp.int32, (picks, choose_top.shape[1]), 1)
    choose_top[...] = jnp.concatenate(
        [(at == names * bands + b).astype(F32) for b in range(bands)], axis=0
    ).astype(BF16)
    results = started(
        [
            (choose_leaf, far_choose_leaf),
            (choose_pair, far_choose_pair),
            (choose_top, far_choose_top),
        ],
        sems,
        len(lists) + leaves,
    )
    broad = cols + 2
    window[...] = jnp.zeros_like(window)
    for g in range(rows):
        start = (g + 1) * broad + 1
        window[start : start + cols] = cells[g * cols : (g + 1) * cols].astype(F32)
    found = jnp.int32(0)
    for at in range(leaves):
        seen = []
        for n in range(count):
            name = listed[n, at // cols, at % cols]
            up, turn = position(name, section, column, rows, cols, width_all)
            where = up * broad + turn
            seen.append(window[where].astype(BF16))
            if n > 0:
                todo[0, found] = (where << 12) + (at << 4) + n
                inside = (up >= 1) & (up <= rows) & (turn >= 1) & (turn <= cols)
                found = found + jnp.where(inside, 0, 1)
        if at % 2 == 0:
            for copy in block_copies[at : at + 2]:
                copy.wait()
        local_part[at] = near_products(seen, blocks.at[at])
    todo[0, todo.shape[1] - 1] = found
    results += started(
        [(todo, far_todo)], sems, len(lists) + leaves + 3
    )
    for copy in results:
        copy.wait()


def chosen(choose, tables, start, count):
    size = choose.shape[1] // 3
    picks = choose.shape[0] // count
    result = jnp.zeros((count * picks, 512), F32)
    for number, table in enumerate(tables):
        result += dot(
            choose[:, number * size : (number + 1) * size], table[start : start + size], NN
        )
    low = lax.broadcasted_iota(jnp.int32, (count, LANES), 1) < RANK
    bands = []
    for n in range(4):
        even, odd = [], []
        for k in range(0, picks, 2):
            one = result[k * count : (k + 1) * count, n * LANES : (n + 1) * LANES]
            two = result[(k + 1) * count : (k + 2) * count, n * LANES : (n + 1) * LANES]
            even.append(jnp.where(low, one, pltpu.roll(two, RANK, 1)))
            odd.append(jnp.where(low, pltpu.roll(one, RANK, 1), two))
        bands += [jnp.concatenate(even, axis=1), jnp.concatenate(odd, axis=1)]
    return jnp.concatenate(bands, axis=0).astype(BF16)


def field_kernel(
    own,
    from_mate,
    from_other,
    local_part,
    far_todo,
    far_choose_leaf,
    far_choose_pair,
    far_choose_top,
    far_emission,
    far_reflect,
    far_couple_leaf,
    far_couple_pair,
    far_blocks,
    parts,
    fields,
    choose_top,
    window,
    todo,
    choose_leaf,
    choose_pair,
    gathered,
    emission,
    reflect,
    couple_leaf,
    couple_pair,
    blocks,
    sems,
    block_sems,
):
    copies = started(
        [
            (far_todo, todo),
            (far_choose_leaf, choose_leaf),
            (far_choose_pair, choose_pair),
            (far_couple_leaf, couple_leaf),
            (far_couple_pair, couple_pair),
            (far_choose_top, choose_top),
            (far_emission, emission),
            (far_reflect, reflect),
        ],
        sems,
    )
    leaves = gathered.shape[0]
    section = lax.axis_index("section")
    bands, rows, cols, leaf = emission.shape
    around = (own.shape[0] - 16 - leaves * 4) // (leaves + cols)
    broad = cols + 2
    width_all = around * cols
    odd = section % 2
    cells_at = around * (leaves + cols)
    sides_at = cells_at + leaves * 4

    def seen_row(source, g, at):
        for p in range(0, cols, 4):
            start = cells_at + (g * cols + p) * 4
            four = source[start : start + 16].astype(F32)
            for k in range(4):
                lanes = slice(k % 2 * leaf, (k % 2 + 1) * leaf)
                window[at * broad + 1 + p + k] = four[k // 2 * 8 : (k // 2 + 1) * 8, lanes]
        two = source[sides_at : sides_at + 16].astype(F32)[:, g * leaf : (g + 1) * leaf]
        window[at * broad] = two[:8]
        window[(at + 1) * broad - 1] = two[8:]

    for g in range(rows):
        seen_row(own, g, g + 1)

    @pl.when(odd == 0)
    def _():
        seen_row(from_other, rows - 1, 0)
        seen_row(from_mate, 0, rows + 1)

    @pl.when(odd == 1)
    def _():
        seen_row(from_mate, rows - 1, 0)
        seen_row(from_other, 0, rows + 1)

    zero_cell = window.shape[0] - 1
    window[zero_cell] = jnp.zeros(window.shape[1:], F32)
    copies[0].wait()

    found = todo[0, todo.shape[1] - 1]

    def block_copy(at, n, slot):
        return pltpu.make_async_copy(
            far_blocks.at[at, n], blocks.at[slot], block_sems.at[slot]
        )

    def fetch(slot, _):
        pair = todo[0, slot]
        block_copy((pair >> 4) & 255, pair & 15, slot).start()
        return 0

    lax.fori_loop(0, found, fetch, 0)
    tables = (own, from_mate, from_other)
    copies[1].wait()
    leaf_pick = chosen(choose_leaf, tables, 0, leaves)
    copies[2].wait()
    pair_pick = chosen(choose_pair, tables, around * leaves, cols)
    split = bands * leaves
    copies[3].wait()
    fields[:split] = own_blocks(dot(leaf_pick, couple_leaf[...], NT), leaves)
    copies[4].wait()
    fields[split:] = own_blocks(dot(pair_pick, couple_pair[...], NT), cols)
    for copy in copies[5:]:
        copy.wait()
    gathered[...] = local_part[...]

    def several(step, _):
        first = step * AT_ONCE
        for k in range(AT_ONCE):

            @pl.when(first + k < found)
            def _():
                block_copy(0, 0, first + k).wait()

        results = []
        for k in range(AT_ONCE):
            slot = jnp.minimum(first + k, found - 1)
            where = jnp.where(first + k < found, todo[0, slot] >> 12, zero_cell)
            cell = window[where].astype(BF16)
            if k % 2 == 0:
                results.append(dot(cell, blocks[slot], NT))
            else:
                results.append(dot(blocks[slot], cell, NT).T)
        for k in range(AT_ONCE):
            at = (todo[0, jnp.minimum(first + k, found - 1)] >> 4) & 255
            gathered[at] += results[k]
        return 0

    lax.fori_loop(0, (found + AT_ONCE - 1) // AT_ONCE, several, 0)
    for g in range(rows):
        near_part = jnp.swapaxes(gathered[g * cols : (g + 1) * cols], 0, 1)
        parts[0, :, g] = emission[:, g] + reflect[:, g] * near_part
        parts[1, :, g] = reflect[:, g]


def result_kernel(tops, parts, fields, choose_top, couple_top, basis, up_leaf, up_pair, out):
    bands, rows, cols, leaf = out.shape
    leaves = rows * cols
    picks = couple_top.shape[1] // RANK
    leaf_field = fields[: bands * leaves, :RANK]
    pair_field = fields[bands * leaves :, :RANK]
    top_pick = dot(choose_top[...], tops[...], NN)
    top_pick = jnp.concatenate([top_pick] * (picks // 2), axis=1)
    kept = row_of(top_pick.shape, picks) == lax.broadcasted_iota(jnp.int32, top_pick.shape, 1) // RANK
    top_pick = jnp.where(kept, top_pick, 0.0).astype(BF16)
    top_field = dot(top_pick, couple_top[...], NT)
    top_field = jnp.sum(top_field.reshape(bands, picks, RANK), axis=1)
    spread = jnp.broadcast_to(top_field[:, None, :], (bands, cols, RANK))
    spread = spread.reshape(bands * cols, RANK).astype(BF16)
    pair_total = pair_field + own_blocks(dot(spread, up_pair[...], NT), cols)[:, :RANK]
    spread = jnp.broadcast_to(
        pair_total.reshape(bands, 1, cols, RANK), (bands, rows, cols, RANK)
    )
    spread = spread.reshape(bands * leaves, RANK).astype(BF16)
    leaf_total = leaf_field + own_blocks(dot(spread, up_leaf[...], NT), leaves)[:, :RANK]
    leaf_total = jnp.concatenate([leaf_total, leaf_total], axis=1)
    far_part = dot(on_diagonal(leaf_total, leaves), basis[...], NN)
    out[...] = parts[0] + parts[1] * far_part.reshape(out.shape)


def body(
    radiosity,
    emission,
    reflect,
    basis,
    up_leaf,
    upward_pair_transfer,
    near_block,
    couple_leaf,
    couple_pair,
    couple_top,
    near_list,
    far_leaf,
    far_pair,
    far_top,
):
    around = lax.axis_size("perim")
    tall = lax.axis_size("section")
    bands, rows, cols, leaf = radiosity.shape
    leaves = rows * cols
    mates = [(s, s ^ 1) for s in range(tall)]
    others = [(s, s + 1 if s % 2 else s - 1) for s in range(1, tall - 1)]
    sems = pltpu.SemaphoreType.DMA
    basis = basis.reshape(leaves * RANK, leaf)
    up_leaf = up_leaf.reshape(leaves * RANK, RANK)
    up_pair = upward_pair_transfer.reshape(cols * RANK, RANK)
    sent, cells = pl.pallas_call(
        coefficients_kernel,
        out_shape=[
            pltpu.HBM((around, 16, WIDE), BF16),
            jax.ShapeDtypeStruct((leaves, bands, leaf), BF16),
        ],
        in_specs=[HBM] * 4,
        out_specs=[HBM, VMEM],
        scratch_shapes=[
            pltpu.VMEM(radiosity.shape, F32),
            pltpu.VMEM(basis.shape, BF16),
            pltpu.VMEM(up_leaf.shape, BF16),
            pltpu.VMEM(up_pair.shape, BF16),
            pltpu.VMEM((2, 16, WIDE), BF16),
            sems((around + 4,)),
        ],
        compiler_params=limit(4),
        name="coefficients",
    )(*map(far, [radiosity, basis, up_leaf, up_pair]))
    ring = lax.all_to_all(sent, "perim", 0, 0)
    blocks = near_block.reshape((leaves,) + near_block.shape[2:])
    couple_leaf = couple_leaf.reshape(leaves * RANK, -1)
    couple_pair = couple_pair.reshape(cols * RANK, -1)
    couple_top = couple_top[0, 0]
    listed = near_list.transpose(2, 0, 1)
    names_leaf = far_leaf.reshape(leaves, -1)
    names_pair = far_pair.reshape(cols, -1)
    names_top = far_top.reshape(1, -1)
    names = [names_leaf, names_pair, names_top]
    window = ((rows + 2) * (cols + 2), bands, leaf)
    choices = [
        pltpu.HBM((names_leaf.size, 3 * around * leaves), BF16),
        pltpu.HBM((names_pair.size, 3 * around * cols), BF16),
        pltpu.HBM((bands * names_top.size, tall * around * bands), BF16),
        pltpu.HBM((1, LANES), jnp.int32),
        jax.ShapeDtypeStruct((leaves, bands, leaf), F32),
    ]
    choose_leaf, choose_pair, choose_top, todo, local_part = pl.pallas_call(
        local_kernel,
        out_shape=choices,
        in_specs=[VMEM] + [HBM] * 5,
        out_specs=[HBM] * 4 + [VMEM],
        scratch_shapes=[
            pltpu.VMEM(window, F32),
            pltpu.SMEM(listed.shape, jnp.int32),
            pltpu.SMEM((1, LANES), jnp.int32),
        ]
        + [pltpu.VMEM(x.shape, x.dtype) for x in names + [blocks] + choices[:3]]
        + [sems((leaves + 9,))],
        compiler_params=limit(17),
        name="local",
    )(cells, *map(far, [listed] + names + [blocks]))
    packed = pl.pallas_call(
        packing_kernel,
        out_shape=jax.ShapeDtypeStruct((around * (leaves + cols) + leaves * 4 + 16, 512), BF16),
        in_specs=[VMEM, VMEM, ANY],
        out_specs=VMEM,
        compiler_params=limit(4),
        name="packing",
    )(ring, cells, local_part)
    tops = pl.pallas_call(
        tops_kernel,
        out_shape=pltpu.HBM((tall, around, bands, LANES), BF16),
        in_specs=[VMEM],
        out_specs=HBM,
        scratch_shapes=[pltpu.VMEM((around, bands, LANES), BF16), sems((tall,))],
        compiler_params=limit(3),
        name="tops",
    )(ring)
    from_mate = lax.ppermute(packed, "section", mates)
    from_other = lax.ppermute(packed, "section", others)
    tops = lax.all_to_all(tops, "section", 0, 0)
    most = leaves * (listed.shape[0] - 1)
    held = [choose_leaf, choose_pair, local_part, emission, reflect, couple_leaf, couple_pair]
    parts, fields, choose_top = pl.pallas_call(
        field_kernel,
        out_shape=[
            jax.ShapeDtypeStruct((2,) + radiosity.shape, F32),
            jax.ShapeDtypeStruct((bands * (leaves + cols), LANES), F32),
            jax.ShapeDtypeStruct(choose_top.shape, BF16),
        ],
        in_specs=[VMEM] * 4 + [HBM] * 9,
        out_specs=[VMEM] * 3,
        scratch_shapes=[
            pltpu.VMEM((window[0] + 1,) + window[1:], F32),
            pltpu.SMEM(todo.shape, jnp.int32),
        ]
        + [pltpu.VMEM(x.shape, x.dtype) for x in held]
        + [pltpu.VMEM((most, leaf, leaf), BF16), sems((9,)), sems((most,))],
        compiler_params=limit(19),
        name="fields",
    )(
        packed,
        from_mate,
        from_other,
        local_part,
        *map(far, [todo] + held[:2] + [choose_top] + held[3:] + [blocks]),
    )
    return pl.pallas_call(
        result_kernel,
        out_shape=jax.ShapeDtypeStruct(radiosity.shape, F32),
        in_specs=[VMEM] * 8,
        out_specs=VMEM,
        compiler_params=limit(4),
        name="result",
    )(
        tops.reshape(tall * around * bands, LANES),
        parts,
        fields,
        choose_top,
        couple_top,
        basis,
        up_leaf,
        up_pair,
    )


def solution(mesh):
    cells = P(None, "section", "perim", None)
    four = P("section", "perim", None, None)
    lists = P("section", "perim", None)
    return jax.shard_map(
        body,
        mesh=mesh,
        in_specs=(cells,) * 3
        + (four,) * 3
        + (P("section", "perim", None, None, None),)
        + (four,) * 3
        + (lists,) * 4,
        out_specs=cells,
        check_vma=False,
    )
```

```python
import jax
import jax.numpy as jnp
from jax import lax
from jax.experimental import pallas as pl
from jax.experimental.pallas import tpu as pltpu
from jax.sharding import PartitionSpec as P

F32 = jnp.float32
BF16 = jnp.bfloat16
NT = (((1,), (1,)), ((), ()))
NN = (((1,), (0,)), ((), ()))
LANES = 128
RANK = 64
WIDE = 1152
VMEM = pl.BlockSpec(memory_space=pltpu.VMEM)
HBM = pl.BlockSpec(memory_space=pltpu.HBM)
ANY = pl.BlockSpec(memory_space=pl.ANY)
AT_ONCE = 16


def dot(left, right, dims):
    return lax.dot_general(left, right, dims, preferred_element_type=F32)


def far(x):
    return pltpu.with_memory_space_constraint(x, pltpu.HBM)


def limit(mib):
    return pltpu.CompilerParams(vmem_limit_bytes=mib * 1024 * 1024)


def row_of(shape, count):
    return lax.broadcasted_iota(jnp.int32, shape, 0) % count


def own_blocks(products, count):
    shape = (products.shape[0], LANES)
    mine = row_of(shape, count) - lax.broadcasted_iota(jnp.int32, shape, 1) // RANK
    total = jnp.zeros(shape, F32)
    for tile in range(count // 2):
        total += jnp.where(mine == 2 * tile, products[:, tile * LANES : (tile + 1) * LANES], 0.0)
    return total + pltpu.roll(total, RANK, 1)


def on_diagonal(twice, count):
    mine = row_of(twice.shape, count) - lax.broadcasted_iota(jnp.int32, twice.shape, 1) // RANK
    tiles = [jnp.where(mine == 2 * tile, twice, 0.0) for tile in range(count // 2)]
    return jnp.concatenate(tiles, axis=1).astype(BF16)


def side_by_side(twice, count):
    low = lax.broadcasted_iota(jnp.int32, (count, LANES), 1) < RANK
    return jnp.concatenate(
        [
            jnp.where(low, twice[b * count : (b + 1) * count], twice[(b + 1) * count : (b + 2) * count])
            for b in range(0, twice.shape[0] // count, 2)
        ],
        axis=1,
    )


def started(copies, sems, at=0):
    made = []
    for number, (source, target) in enumerate(copies):
        made.append(pltpu.make_async_copy(source, target, sems.at[at + number]))
        made[-1].start()
    return made


def coefficients_kernel(
    far_radiosity,
    far_basis,
    far_up_leaf,
    far_up_pair,
    sent,
    cells,
    radiosity,
    basis,
    up_leaf,
    up_pair,
    block,
    sems,
):
    copies = started(
        [
            (far_radiosity, radiosity),
            (far_basis, basis),
            (far_up_leaf, up_leaf),
            (far_up_pair, up_pair),
        ],
        sems,
    )
    copies[0].wait()
    column = lax.axis_index("perim")
    bands, rows, cols, leaf = radiosity.shape
    leaves = rows * cols
    shaded = radiosity[...].reshape(bands * leaves, leaf).astype(BF16)
    copies[1].wait()
    leaf_twice = own_blocks(dot(shaded, basis[...], NT), leaves)
    of_pairs = leaf_twice.reshape(bands, rows, cols, LANES)
    of_pairs = jnp.concatenate(
        [on_diagonal(of_pairs[:, g].reshape(bands * cols, LANES), cols) for g in range(rows)],
        axis=1,
    )
    copies[2].wait()
    pair = dot(of_pairs, up_leaf[...], NN)
    pair_twice = jnp.concatenate([pair, pair], axis=1)
    copies[3].wait()
    top = dot(on_diagonal(pair_twice, cols), up_pair[...], NN)
    top = jnp.sum(top.reshape(bands, cols, RANK), axis=1)
    top_twice = jnp.concatenate([top, top], axis=1)

    def edge(col):
        return jnp.concatenate(
            [radiosity[:, g, col, :] for g in range(rows)], axis=1
        )

    leaf_part = side_by_side(leaf_twice, leaves)
    pair_part = side_by_side(pair_twice, cols)
    top_part = jnp.concatenate([top_twice, jnp.zeros_like(top_twice)], axis=0)

    for right, col in enumerate((0, cols - 1)):
        block[right] = jnp.concatenate(
            [leaf_part, jnp.concatenate([pair_part, edge(col)], axis=0), top_part], axis=1
        ).astype(BF16)
    around = sent.shape[0]
    to_right = (column + 1) % around
    copies = started(
        [(block.at[jnp.where(to_right == to, 1, 0)], sent.at[to]) for to in range(around)], sems, 4
    )
    for g in range(rows):
        turned = jnp.swapaxes(radiosity[:, g], 0, 1)
        cells[g * cols : (g + 1) * cols] = turned.astype(BF16)
    for copy in copies:
        copy.wait()


def packing_kernel(ring, cells, local_part, packed):
    column = lax.axis_index("perim")
    around, leaves = ring.shape[:2]
    cols = leaves // 2
    for at in range(around):
        packed[at * leaves : (at + 1) * leaves] = ring[at, :, :512]
    for at in range(0, around, 2):
        start = around * leaves + at * cols
        both = [ring[at + k, :, 512:1024].astype(F32)[:cols] for k in range(2)]
        packed[start : start + 2 * cols] = jnp.concatenate(both, axis=0).astype(BF16)
    start = around * (leaves + cols)
    for at in range(0, leaves, 4):
        four = [cells[at + k].astype(F32) for k in range(4)]
        two = [jnp.concatenate(four[:2], axis=1), jnp.concatenate(four[2:], axis=1)]
        packed[start + at * 4 : start + at * 4 + 16] = jnp.concatenate(two, axis=0).astype(BF16)
    start += leaves * 4
    sides = [(column + around - 1) % around, (column + 1) % around]
    both = [ring[at, :, 512:1024].astype(F32)[8:] for at in sides]
    packed[start : start + 16] = jnp.concatenate(both, axis=0).astype(BF16)


def tops_kernel(ring, tops, row_tops, sems):
    row_tops[...] = ring[:, :8, 1024:]
    for copy in started([(row_tops, tops.at[to]) for to in range(tops.shape[0])], sems):
        copy.wait()


def one_hot(tier, inner, size):
    count, picks = inner.shape
    slots = tier * size + inner
    at = lax.broadcasted_iota(jnp.int32, (count, 3 * size), 1)
    return jnp.concatenate(
        [(at == slots[:, k : k + 1]).astype(F32) for k in range(picks)], axis=0
    ).astype(BF16)


def near_products(seen, blocks):
    total = jnp.zeros(seen[0].shape, F32)
    turned = jnp.zeros(seen[0].shape[::-1], F32)
    for n, cell in enumerate(seen):
        if n % 2 == 0:
            total += dot(cell, blocks[n], NT)
        else:
            turned += dot(blocks[n], cell, NT)
    return total + turned.T


def split_name(name, width_all):
    if width_all & (width_all - 1):
        return name // width_all, name % width_all
    return name >> (width_all.bit_length() - 1), name & (width_all - 1)


def position(name, section, column, rows, cols, width_all):
    row = split_name(name, width_all)[0]
    turn = split_name(name + (width_all + 1 - cols * column), width_all)[1]
    return row - (rows * section - 1), turn


def local_kernel(
    cells,
    far_listed,
    far_names_leaf,
    far_names_pair,
    far_names_top,
    far_blocks,
    far_choose_leaf,
    far_choose_pair,
    far_choose_top,
    far_todo,
    local_part,
    window,
    listed,
    todo,
    names_leaf,
    names_pair,
    names_top,
    blocks,
    choose_leaf,
    choose_pair,
    choose_top,
    sems,
):
    leaves, count = blocks.shape[:2]
    lists = started(
        [
            (far_names_leaf, names_leaf),
            (far_names_pair, names_pair),
            (far_names_top, names_top),
            (far_listed, listed),
        ],
        sems,
    )
    block_copies = started(
        [(far_blocks.at[at], blocks.at[at]) for at in range(leaves)], sems, len(lists)
    )
    for copy in lists:
        copy.wait()
    section, column = lax.axis_index("section"), lax.axis_index("perim")
    cols = names_pair.shape[0]
    rows = leaves // cols
    width_all = choose_pair.shape[1] // 3
    mate = section + 1 - 2 * (section % 2)

    def tier_of(source):
        return jnp.where(source == section, 0, jnp.where(source == mate, 1, 2))

    names = names_leaf[...]
    height, turn = split_name(names, width_all)
    source, height = split_name(height, rows)
    device, turn = split_name(turn, cols)
    choose_leaf[...] = one_hot(
        tier_of(source), device * leaves + height * cols + turn, width_all * rows
    )
    height, turn = split_name(names_pair[...], width_all)
    choose_pair[...] = one_hot(tier_of(height), turn, width_all)
    picks = names_top.shape[1]
    bands = choose_top.shape[0] // picks
    square = (picks, picks)
    names = jnp.broadcast_to(names_top[...], square)
    diagonal = lax.broadcasted_iota(jnp.int32, square, 0) == lax.broadcasted_iota(jnp.int32, square, 1)
    names = jnp.sum(jnp.where(diagonal, names, 0), axis=1, keepdims=True)
    at = lax.broadcasted_iota(jnp.int32, (picks, choose_top.shape[1]), 1)
    choose_top[...] = jnp.concatenate(
        [(at == names * bands + b).astype(F32) for b in range(bands)], axis=0
    ).astype(BF16)
    results = started(
        [
            (choose_leaf, far_choose_leaf),
            (choose_pair, far_choose_pair),
            (choose_top, far_choose_top),
        ],
        sems,
        len(lists) + leaves,
    )
    broad = cols + 2
    window[...] = jnp.zeros_like(window)
    for g in range(rows):
        start = (g + 1) * broad + 1
        window[start : start + cols] = cells[g * cols : (g + 1) * cols].astype(F32)
    found = jnp.int32(0)
    for at in range(leaves):
        seen = []
        for n in range(count):
            name = listed[n, at // cols, at % cols]
            up, turn = position(name, section, column, rows, cols, width_all)
            where = up * broad + turn
            seen.append(window[where].astype(BF16))
            if n > 0:
                todo[0, found] = (where << 12) + (at << 4) + n
                inside = (up >= 1) & (up <= rows) & (turn >= 1) & (turn <= cols)
                found = found + jnp.where(inside, 0, 1)
        if at % 2 == 0:
            for copy in block_copies[at : at + 2]:
                copy.wait()
        local_part[at] = near_products(seen, blocks.at[at])
    todo[0, todo.shape[1] - 1] = found
    results += started(
        [(todo, far_todo)], sems, len(lists) + leaves + 3
    )
    for copy in results:
        copy.wait()


def chosen(choose, tables, start, count):
    size = choose.shape[1] // 3
    picks = choose.shape[0] // count
    result = jnp.zeros((count * picks, 512), F32)
    for number, table in enumerate(tables):
        result += dot(
            choose[:, number * size : (number + 1) * size], table[start : start + size], NN
        )
    low = lax.broadcasted_iota(jnp.int32, (count, LANES), 1) < RANK
    bands = []
    for n in range(4):
        even, odd = [], []
        for k in range(0, picks, 2):
            one = result[k * count : (k + 1) * count, n * LANES : (n + 1) * LANES]
            two = result[(k + 1) * count : (k + 2) * count, n * LANES : (n + 1) * LANES]
            even.append(jnp.where(low, one, pltpu.roll(two, RANK, 1)))
            odd.append(jnp.where(low, pltpu.roll(one, RANK, 1), two))
        bands += [jnp.concatenate(even, axis=1), jnp.concatenate(odd, axis=1)]
    return jnp.concatenate(bands, axis=0).astype(BF16)


def field_kernel(
    own,
    from_mate,
    from_other,
    local_part,
    far_todo,
    far_choose_leaf,
    far_choose_pair,
    far_couple_leaf,
    far_couple_pair,
    far_blocks,
    gathered,
    fields,
    window,
    todo,
    choose_leaf,
    choose_pair,
    couple_leaf,
    couple_pair,
    blocks,
    sems,
    block_sems,
):
    copies = started(
        [
            (far_todo, todo),
            (far_choose_leaf, choose_leaf),
            (far_choose_pair, choose_pair),
            (far_couple_leaf, couple_leaf),
            (far_couple_pair, couple_pair),
        ],
        sems,
    )
    leaves = gathered.shape[0]
    section = lax.axis_index("section")
    bands, leaf = gathered.shape[1:]
    cols = fields.shape[0] // bands - leaves
    rows = leaves // cols
    around = (own.shape[0] - 16 - leaves * 4) // (leaves + cols)
    broad = cols + 2
    width_all = around * cols
    odd = section % 2
    cells_at = around * (leaves + cols)
    sides_at = cells_at + leaves * 4

    def seen_row(source, g, at):
        for p in range(0, cols, 4):
            start = cells_at + (g * cols + p) * 4
            four = source[start : start + 16].astype(F32)
            for k in range(4):
                lanes = slice(k % 2 * leaf, (k % 2 + 1) * leaf)
                window[at * broad + 1 + p + k] = four[k // 2 * 8 : (k // 2 + 1) * 8, lanes]
        two = source[sides_at : sides_at + 16].astype(F32)[:, g * leaf : (g + 1) * leaf]
        window[at * broad] = two[:8]
        window[(at + 1) * broad - 1] = two[8:]

    for g in range(rows):
        seen_row(own, g, g + 1)

    @pl.when(odd == 0)
    def _():
        seen_row(from_other, rows - 1, 0)
        seen_row(from_mate, 0, rows + 1)

    @pl.when(odd == 1)
    def _():
        seen_row(from_mate, rows - 1, 0)
        seen_row(from_other, 0, rows + 1)

    zero_cell = window.shape[0] - 1
    window[zero_cell] = jnp.zeros(window.shape[1:], F32)
    copies[0].wait()

    found = todo[0, todo.shape[1] - 1]

    def block_copy(at, n, slot):
        return pltpu.make_async_copy(
            far_blocks.at[at, n], blocks.at[slot], block_sems.at[slot]
        )

    def fetch(step, _):
        for k in range(4):
            slot = 4 * step + k

            @pl.when(slot < found)
            def _():
                pair = todo[0, slot]
                block_copy((pair >> 4) & 255, pair & 15, slot).start()

        return 0

    lax.fori_loop(0, (found + 3) // 4, fetch, 0)
    tables = (own, from_mate, from_other)
    copies[1].wait()
    leaf_pick = chosen(choose_leaf, tables, 0, leaves)
    copies[2].wait()
    pair_pick = chosen(choose_pair, tables, around * leaves, cols)
    split = bands * leaves
    copies[3].wait()
    fields[:split] = own_blocks(dot(leaf_pick, couple_leaf[...], NT), leaves)
    copies[4].wait()
    fields[split:] = own_blocks(dot(pair_pick, couple_pair[...], NT), cols)
    gathered[...] = local_part[...]

    def several(step, _):
        first = step * AT_ONCE
        for k in range(AT_ONCE):

            @pl.when(first + k < found)
            def _():
                block_copy(0, 0, first + k).wait()

        results = []
        for k in range(AT_ONCE):
            slot = jnp.minimum(first + k, found - 1)
            where = jnp.where(first + k < found, todo[0, slot] >> 12, zero_cell)
            cell = window[where].astype(BF16)
            if k % 2 == 0:
                results.append(dot(cell, blocks[slot], NT))
            else:
                results.append(dot(blocks[slot], cell, NT).T)
        for k in range(AT_ONCE):
            at = (todo[0, jnp.minimum(first + k, found - 1)] >> 4) & 255
            gathered[at] += results[k]
        return 0

    lax.fori_loop(0, (found + AT_ONCE - 1) // AT_ONCE, several, 0)


def result_kernel(
    tops, gathered, fields, choose_top, couple_top, basis, up_leaf, up_pair, emission, reflect, out
):
    bands, rows, cols, leaf = out.shape
    leaves = rows * cols
    picks = couple_top.shape[1] // RANK
    leaf_field = fields[: bands * leaves, :RANK]
    pair_field = fields[bands * leaves :, :RANK]
    top_pick = dot(choose_top[...], tops[...], NN)
    top_pick = jnp.concatenate([top_pick] * (picks // 2), axis=1)
    kept = row_of(top_pick.shape, picks) == lax.broadcasted_iota(jnp.int32, top_pick.shape, 1) // RANK
    top_pick = jnp.where(kept, top_pick, 0.0).astype(BF16)
    top_field = dot(top_pick, couple_top[...], NT)
    top_field = jnp.sum(top_field.reshape(bands, picks, RANK), axis=1)
    spread = jnp.broadcast_to(top_field[:, None, :], (bands, cols, RANK))
    spread = spread.reshape(bands * cols, RANK).astype(BF16)
    pair_total = pair_field + own_blocks(dot(spread, up_pair[...], NT), cols)[:, :RANK]
    spread = jnp.broadcast_to(
        pair_total.reshape(bands, 1, cols, RANK), (bands, rows, cols, RANK)
    )
    spread = spread.reshape(bands * leaves, RANK).astype(BF16)
    leaf_total = leaf_field + own_blocks(dot(spread, up_leaf[...], NT), leaves)[:, :RANK]
    leaf_total = jnp.concatenate([leaf_total, leaf_total], axis=1)
    far_part = dot(on_diagonal(leaf_total, leaves), basis[...], NN)
    far_part = far_part.reshape(out.shape)
    for g in range(rows):
        near_part = jnp.swapaxes(gathered[g * cols : (g + 1) * cols], 0, 1)
        out[:, g] = emission[:, g] + reflect[:, g] * (near_part + far_part[:, g])


def body(
    radiosity,
    emission,
    reflect,
    basis,
    up_leaf,
    upward_pair_transfer,
    near_block,
    couple_leaf,
    couple_pair,
    couple_top,
    near_list,
    far_leaf,
    far_pair,
    far_top,
):
    around = lax.axis_size("perim")
    tall = lax.axis_size("section")
    bands, rows, cols, leaf = radiosity.shape
    leaves = rows * cols
    mates = [(s, s ^ 1) for s in range(tall)]
    others = [(s, s + 1 if s % 2 else s - 1) for s in range(1, tall - 1)]
    sems = pltpu.SemaphoreType.DMA
    basis = basis.reshape(leaves * RANK, leaf)
    up_leaf = up_leaf.reshape(leaves * RANK, RANK)
    up_pair = upward_pair_transfer.reshape(cols * RANK, RANK)
    sent, cells = pl.pallas_call(
        coefficients_kernel,
        out_shape=[
            pltpu.HBM((around, 16, WIDE), BF16),
            jax.ShapeDtypeStruct((leaves, bands, leaf), BF16),
        ],
        in_specs=[HBM] * 4,
        out_specs=[HBM, VMEM],
        scratch_shapes=[
            pltpu.VMEM(radiosity.shape, F32),
            pltpu.VMEM(basis.shape, BF16),
            pltpu.VMEM(up_leaf.shape, BF16),
            pltpu.VMEM(up_pair.shape, BF16),
            pltpu.VMEM((2, 16, WIDE), BF16),
            sems((around + 4,)),
        ],
        compiler_params=limit(4),
        name="coefficients",
    )(*map(far, [radiosity, basis, up_leaf, up_pair]))
    ring = lax.all_to_all(sent, "perim", 0, 0)
    blocks = near_block.reshape((leaves,) + near_block.shape[2:])
    couple_leaf = couple_leaf.reshape(leaves * RANK, -1)
    couple_pair = couple_pair.reshape(cols * RANK, -1)
    couple_top = couple_top[0, 0]
    listed = near_list.transpose(2, 0, 1)
    names_leaf = far_leaf.reshape(leaves, -1)
    names_pair = far_pair.reshape(cols, -1)
    names_top = far_top.reshape(1, -1)
    names = [names_leaf, names_pair, names_top]
    window = ((rows + 2) * (cols + 2), bands, leaf)
    choices = [
        pltpu.HBM((names_leaf.size, 3 * around * leaves), BF16),
        pltpu.HBM((names_pair.size, 3 * around * cols), BF16),
        pltpu.HBM((bands * names_top.size, tall * around * bands), BF16),
        pltpu.HBM((1, LANES), jnp.int32),
        jax.ShapeDtypeStruct((leaves, bands, leaf), F32),
    ]
    choose_leaf, choose_pair, choose_top, todo, local_part = pl.pallas_call(
        local_kernel,
        out_shape=choices,
        in_specs=[VMEM] + [HBM] * 5,
        out_specs=[HBM] * 4 + [VMEM],
        scratch_shapes=[
            pltpu.VMEM(window, F32),
            pltpu.SMEM(listed.shape, jnp.int32),
            pltpu.SMEM((1, LANES), jnp.int32),
        ]
        + [pltpu.VMEM(x.shape, x.dtype) for x in names + [blocks] + choices[:3]]
        + [sems((leaves + 9,))],
        compiler_params=limit(17),
        name="local",
    )(cells, *map(far, [listed] + names + [blocks]))
    packed = pl.pallas_call(
        packing_kernel,
        out_shape=jax.ShapeDtypeStruct((around * (leaves + cols) + leaves * 4 + 16, 512), BF16),
        in_specs=[VMEM, VMEM, ANY],
        out_specs=VMEM,
        compiler_params=limit(4),
        name="packing",
    )(ring, cells, local_part)
    tops = pl.pallas_call(
        tops_kernel,
        out_shape=pltpu.HBM((tall, around, bands, LANES), BF16),
        in_specs=[VMEM],
        out_specs=HBM,
        scratch_shapes=[pltpu.VMEM((around, bands, LANES), BF16), sems((tall,))],
        compiler_params=limit(3),
        name="tops",
    )(ring)
    from_mate = lax.ppermute(packed, "section", mates)
    from_other = lax.ppermute(packed, "section", others)
    tops = lax.all_to_all(tops, "section", 0, 0)
    most = leaves * (listed.shape[0] - 1)
    held = [choose_leaf, choose_pair, couple_leaf, couple_pair]
    gathered, fields = pl.pallas_call(
        field_kernel,
        out_shape=[
            jax.ShapeDtypeStruct((leaves, bands, leaf), F32),
            jax.ShapeDtypeStruct((bands * (leaves + cols), LANES), F32),
        ],
        in_specs=[VMEM] * 4 + [HBM] * 6,
        out_specs=[VMEM] * 2,
        scratch_shapes=[
            pltpu.VMEM((window[0] + 1,) + window[1:], F32),
            pltpu.SMEM(todo.shape, jnp.int32),
        ]
        + [pltpu.VMEM(x.shape, x.dtype) for x in held]
        + [pltpu.VMEM((most, leaf, leaf), BF16), sems((5,)), sems((most,))],
        compiler_params=limit(19),
        name="fields",
    )(
        packed,
        from_mate,
        from_other,
        local_part,
        *map(far, [todo] + held + [blocks]),
    )
    return pl.pallas_call(
        result_kernel,
        out_shape=jax.ShapeDtypeStruct(radiosity.shape, F32),
        in_specs=[VMEM] * 10,
        out_specs=VMEM,
        compiler_params=limit(4),
        name="result",
    )(
        tops.reshape(tall * around * bands, LANES),
        gathered,
        fields,
        choose_top,
        couple_top,
        basis,
        up_leaf,
        up_pair,
        emission,
        reflect,
    )


def solution(mesh):
    cells = P(None, "section", "perim", None)
    four = P("section", "perim", None, None)
    lists = P("section", "perim", None)
    return jax.shard_map(
        body,
        mesh=mesh,
        in_specs=(cells,) * 3
        + (four,) * 3
        + (P("section", "perim", None, None, None),)
        + (four,) * 3
        + (lists,) * 4,
        out_specs=cells,
        check_vma=False,
    )
```

```python
import jax
import jax.numpy as jnp
from jax import lax
from jax.experimental import pallas as pl
from jax.experimental.pallas import tpu as pltpu
from jax.sharding import PartitionSpec as P

F32 = jnp.float32
BF16 = jnp.bfloat16
NT = (((1,), (1,)), ((), ()))
NN = (((1,), (0,)), ((), ()))
LANES = 128
RANK = 64
WIDE = 1152
VMEM = pl.BlockSpec(memory_space=pltpu.VMEM)
HBM = pl.BlockSpec(memory_space=pltpu.HBM)
ANY = pl.BlockSpec(memory_space=pl.ANY)
AT_ONCE = 16


def dot(left, right, dims):
    return lax.dot_general(left, right, dims, preferred_element_type=F32)


def far(x):
    return pltpu.with_memory_space_constraint(x, pltpu.HBM)


def limit(mib):
    return pltpu.CompilerParams(vmem_limit_bytes=mib * 1024 * 1024)


def row_of(shape, count):
    return lax.broadcasted_iota(jnp.int32, shape, 0) % count


def own_blocks(products, count):
    shape = (products.shape[0], LANES)
    mine = row_of(shape, count) - lax.broadcasted_iota(jnp.int32, shape, 1) // RANK
    total = jnp.zeros(shape, F32)
    for tile in range(count // 2):
        total += jnp.where(mine == 2 * tile, products[:, tile * LANES : (tile + 1) * LANES], 0.0)
    return total + pltpu.roll(total, RANK, 1)


def on_diagonal(twice, count):
    mine = row_of(twice.shape, count) - lax.broadcasted_iota(jnp.int32, twice.shape, 1) // RANK
    tiles = [jnp.where(mine == 2 * tile, twice, 0.0) for tile in range(count // 2)]
    return jnp.concatenate(tiles, axis=1).astype(BF16)


def side_by_side(twice, count):
    low = lax.broadcasted_iota(jnp.int32, (count, LANES), 1) < RANK
    return jnp.concatenate(
        [
            jnp.where(low, twice[b * count : (b + 1) * count], twice[(b + 1) * count : (b + 2) * count])
            for b in range(0, twice.shape[0] // count, 2)
        ],
        axis=1,
    )


def started(copies, sems, at=0):
    made = []
    for number, (source, target) in enumerate(copies):
        made.append(pltpu.make_async_copy(source, target, sems.at[at + number]))
        made[-1].start()
    return made


def coefficients_kernel(
    far_radiosity,
    far_basis,
    far_up_leaf,
    far_up_pair,
    sent,
    cells,
    radiosity,
    basis,
    up_leaf,
    up_pair,
    block,
    sems,
):
    copies = started(
        [
            (far_radiosity, radiosity),
            (far_basis, basis),
            (far_up_leaf, up_leaf),
            (far_up_pair, up_pair),
        ],
        sems,
    )
    copies[0].wait()
    column = lax.axis_index("perim")
    bands, rows, cols, leaf = radiosity.shape
    leaves = rows * cols
    shaded = radiosity[...].reshape(bands * leaves, leaf).astype(BF16)
    copies[1].wait()
    leaf_twice = own_blocks(dot(shaded, basis[...], NT), leaves)
    of_pairs = leaf_twice.reshape(bands, rows, cols, LANES)
    of_pairs = jnp.concatenate(
        [on_diagonal(of_pairs[:, g].reshape(bands * cols, LANES), cols) for g in range(rows)],
        axis=1,
    )
    copies[2].wait()
    pair = dot(of_pairs, up_leaf[...], NN)
    pair_twice = jnp.concatenate([pair, pair], axis=1)
    copies[3].wait()
    top = dot(on_diagonal(pair_twice, cols), up_pair[...], NN)
    top = jnp.sum(top.reshape(bands, cols, RANK), axis=1)
    top_twice = jnp.concatenate([top, top], axis=1)

    def edge(col):
        return jnp.concatenate(
            [radiosity[:, g, col, :] for g in range(rows)], axis=1
        )

    leaf_part = side_by_side(leaf_twice, leaves)
    pair_part = side_by_side(pair_twice, cols)
    top_part = jnp.concatenate([top_twice, jnp.zeros_like(top_twice)], axis=0)

    for right, col in enumerate((0, cols - 1)):
        block[right] = jnp.concatenate(
            [leaf_part, jnp.concatenate([pair_part, edge(col)], axis=0), top_part], axis=1
        ).astype(BF16)
    around = sent.shape[0]
    to_right = (column + 1) % around
    copies = started(
        [(block.at[jnp.where(to_right == to, 1, 0)], sent.at[to]) for to in range(around)], sems, 4
    )
    for g in range(rows):
        turned = jnp.swapaxes(radiosity[:, g], 0, 1)
        cells[g * cols : (g + 1) * cols] = turned.astype(BF16)
    for copy in copies:
        copy.wait()


def packing_kernel(ring, cells, local_part, packed):
    column = lax.axis_index("perim")
    around, leaves = ring.shape[:2]
    cols = leaves // 2
    for at in range(around):
        packed[at * leaves : (at + 1) * leaves] = ring[at, :, :512]
    for at in range(0, around, 2):
        start = around * leaves + at * cols
        both = [ring[at + k, :, 512:1024].astype(F32)[:cols] for k in range(2)]
        packed[start : start + 2 * cols] = jnp.concatenate(both, axis=0).astype(BF16)
    start = around * (leaves + cols)
    for at in range(0, leaves, 4):
        four = [cells[at + k].astype(F32) for k in range(4)]
        two = [jnp.concatenate(four[:2], axis=1), jnp.concatenate(four[2:], axis=1)]
        packed[start + at * 4 : start + at * 4 + 16] = jnp.concatenate(two, axis=0).astype(BF16)
    start += leaves * 4
    sides = [(column + around - 1) % around, (column + 1) % around]
    both = [ring[at, :, 512:1024].astype(F32)[8:] for at in sides]
    packed[start : start + 16] = jnp.concatenate(both, axis=0).astype(BF16)


def tops_kernel(ring, tops, row_tops, sems):
    rows = ring[:, :, 1024:].astype(F32)[:, :8]
    row_tops[...] = rows.reshape(row_tops.shape).astype(BF16)
    for copy in started([(row_tops, tops.at[to]) for to in range(tops.shape[0])], sems):
        copy.wait()


def one_hot(tier, inner, size):
    count, picks = inner.shape
    slots = tier * size + inner
    at = lax.broadcasted_iota(jnp.int32, (count, 3 * size), 1)
    return jnp.concatenate(
        [(at == slots[:, k : k + 1]).astype(F32) for k in range(picks)], axis=0
    ).astype(BF16)


def near_products(seen, blocks):
    total = jnp.zeros(seen[0].shape, F32)
    turned = jnp.zeros(seen[0].shape[::-1], F32)
    for n, cell in enumerate(seen):
        if n % 2 == 0:
            total += dot(cell, blocks[n], NT)
        else:
            turned += dot(blocks[n], cell, NT)
    return total + turned.T


def split_name(name, width_all):
    if width_all & (width_all - 1):
        return name // width_all, name % width_all
    return name >> (width_all.bit_length() - 1), name & (width_all - 1)


def position(name, section, column, rows, cols, width_all):
    row = split_name(name, width_all)[0]
    turn = split_name(name + (width_all + 1 - cols * column), width_all)[1]
    return row - (rows * section - 1), turn


def local_kernel(
    cells,
    far_listed,
    far_names_leaf,
    far_names_pair,
    far_names_top,
    far_blocks,
    far_choose_leaf,
    far_choose_pair,
    far_choose_top,
    far_todo,
    local_part,
    window,
    listed,
    todo,
    names_leaf,
    names_pair,
    names_top,
    blocks,
    choose_leaf,
    choose_pair,
    choose_top,
    sems,
):
    leaves, count = blocks.shape[:2]
    lists = started(
        [
            (far_names_leaf, names_leaf),
            (far_names_pair, names_pair),
            (far_names_top, names_top),
            (far_listed, listed),
        ],
        sems,
    )
    block_copies = started(
        [(far_blocks.at[at], blocks.at[at]) for at in range(leaves)], sems, len(lists)
    )
    for copy in lists:
        copy.wait()
    section, column = lax.axis_index("section"), lax.axis_index("perim")
    cols = names_pair.shape[0]
    rows = leaves // cols
    width_all = choose_pair.shape[1] // 3
    mate = section + 1 - 2 * (section % 2)

    def tier_of(source):
        return jnp.where(source == section, 0, jnp.where(source == mate, 1, 2))

    names = names_leaf[...]
    height, turn = split_name(names, width_all)
    source, height = split_name(height, rows)
    device, turn = split_name(turn, cols)
    choose_leaf[...] = one_hot(
        tier_of(source), device * leaves + height * cols + turn, width_all * rows
    )
    height, turn = split_name(names_pair[...], width_all)
    choose_pair[...] = one_hot(tier_of(height), turn, width_all)
    picks = names_top.shape[1]
    bands = choose_top.shape[0] // picks
    square = (picks, picks)
    names = jnp.broadcast_to(names_top[...], square)
    diagonal = lax.broadcasted_iota(jnp.int32, square, 0) == lax.broadcasted_iota(jnp.int32, square, 1)
    names = jnp.sum(jnp.where(diagonal, names, 0), axis=1, keepdims=True)
    at = lax.broadcasted_iota(jnp.int32, (picks, choose_top.shape[1]), 1)
    choose_top[...] = jnp.concatenate(
        [(at == names * bands + b).astype(F32) for b in range(bands)], axis=0
    ).astype(BF16)
    results = started(
        [
            (choose_leaf, far_choose_leaf),
            (choose_pair, far_choose_pair),
            (choose_top, far_choose_top),
        ],
        sems,
        len(lists) + leaves,
    )
    broad = cols + 2
    window[...] = jnp.zeros_like(window)
    for g in range(rows):
        start = (g + 1) * broad + 1
        window[start : start + cols] = cells[g * cols : (g + 1) * cols].astype(F32)
    found = jnp.int32(0)
    for at in range(leaves):
        seen = []
        for n in range(count):
            name = listed[n, at // cols, at % cols]
            up, turn = position(name, section, column, rows, cols, width_all)
            where = up * broad + turn
            seen.append(window[where].astype(BF16))
            if n > 0:
                todo[0, found] = (where << 12) + (at << 4) + n
                inside = (up >= 1) & (up <= rows) & (turn >= 1) & (turn <= cols)
                found = found + jnp.where(inside, 0, 1)
        if at % 2 == 0:
            for copy in block_copies[at : at + 2]:
                copy.wait()
        local_part[at] = near_products(seen, blocks.at[at])
    todo[0, todo.shape[1] - 1] = found
    results += started(
        [(todo, far_todo)], sems, len(lists) + leaves + 3
    )
    for copy in results:
        copy.wait()


def chosen(choose, tables, start, count):
    size = choose.shape[1] // 3
    picks = choose.shape[0] // count
    result = jnp.zeros((count * picks, 512), F32)
    for number, table in enumerate(tables):
        result += dot(
            choose[:, number * size : (number + 1) * size], table[start : start + size], NN
        )
    low = lax.broadcasted_iota(jnp.int32, (count, LANES), 1) < RANK
    bands = []
    for n in range(4):
        even, odd = [], []
        for k in range(0, picks, 2):
            one = result[k * count : (k + 1) * count, n * LANES : (n + 1) * LANES]
            two = result[(k + 1) * count : (k + 2) * count, n * LANES : (n + 1) * LANES]
            even.append(jnp.where(low, one, pltpu.roll(two, RANK, 1)))
            odd.append(jnp.where(low, pltpu.roll(one, RANK, 1), two))
        bands += [jnp.concatenate(even, axis=1), jnp.concatenate(odd, axis=1)]
    return jnp.concatenate(bands, axis=0).astype(BF16)


def field_kernel(
    own,
    from_mate,
    from_other,
    local_part,
    far_todo,
    far_choose_leaf,
    far_choose_pair,
    far_couple_leaf,
    far_couple_pair,
    far_blocks,
    gathered,
    fields,
    window,
    todo,
    choose_leaf,
    choose_pair,
    couple_leaf,
    couple_pair,
    blocks,
    sems,
    block_sems,
):
    copies = started(
        [
            (far_todo, todo),
            (far_choose_leaf, choose_leaf),
            (far_choose_pair, choose_pair),
            (far_couple_leaf, couple_leaf),
            (far_couple_pair, couple_pair),
        ],
        sems,
    )
    leaves = gathered.shape[0]
    section = lax.axis_index("section")
    bands, leaf = gathered.shape[1:]
    cols = fields.shape[0] // bands - leaves
    rows = leaves // cols
    around = (own.shape[0] - 16 - leaves * 4) // (leaves + cols)
    broad = cols + 2
    width_all = around * cols
    odd = section % 2
    cells_at = around * (leaves + cols)
    sides_at = cells_at + leaves * 4

    def seen_row(source, g, at):
        for p in range(0, cols, 4):
            start = cells_at + (g * cols + p) * 4
            four = source[start : start + 16].astype(F32)
            for k in range(4):
                lanes = slice(k % 2 * leaf, (k % 2 + 1) * leaf)
                window[at * broad + 1 + p + k] = four[k // 2 * 8 : (k // 2 + 1) * 8, lanes]
        two = source[sides_at : sides_at + 16].astype(F32)[:, g * leaf : (g + 1) * leaf]
        window[at * broad] = two[:8]
        window[(at + 1) * broad - 1] = two[8:]

    for g in range(rows):
        seen_row(own, g, g + 1)

    @pl.when(odd == 0)
    def _():
        seen_row(from_other, rows - 1, 0)
        seen_row(from_mate, 0, rows + 1)

    @pl.when(odd == 1)
    def _():
        seen_row(from_mate, rows - 1, 0)
        seen_row(from_other, 0, rows + 1)

    zero_cell = window.shape[0] - 1
    window[zero_cell] = jnp.zeros(window.shape[1:], F32)
    copies[0].wait()

    found = todo[0, todo.shape[1] - 1]

    def block_copy(at, n, slot):
        return pltpu.make_async_copy(
            far_blocks.at[at, n], blocks.at[slot], block_sems.at[slot]
        )

    def fetch(step, _):
        for k in range(4):
            slot = 4 * step + k

            @pl.when(slot < found)
            def _():
                pair = todo[0, slot]
                block_copy((pair >> 4) & 255, pair & 15, slot).start()

        return 0

    lax.fori_loop(0, (found + 3) // 4, fetch, 0)
    tables = (own, from_mate, from_other)
    copies[1].wait()
    leaf_pick = chosen(choose_leaf, tables, 0, leaves)
    copies[2].wait()
    pair_pick = chosen(choose_pair, tables, around * leaves, cols)
    split = bands * leaves
    copies[3].wait()
    fields[:split] = own_blocks(dot(leaf_pick, couple_leaf[...], NT), leaves)
    copies[4].wait()
    fields[split:] = own_blocks(dot(pair_pick, couple_pair[...], NT), cols)
    gathered[...] = local_part[...]

    def several(step, _):
        first = step * AT_ONCE
        for k in range(AT_ONCE):

            @pl.when(first + k < found)
            def _():
                block_copy(0, 0, first + k).wait()

        results = []
        for k in range(AT_ONCE):
            slot = jnp.minimum(first + k, found - 1)
            where = jnp.where(first + k < found, todo[0, slot] >> 12, zero_cell)
            cell = window[where].astype(BF16)
            if k % 2 == 0:
                results.append(dot(cell, blocks[slot], NT))
            else:
                results.append(dot(blocks[slot], cell, NT).T)
        for k in range(AT_ONCE):
            at = (todo[0, jnp.minimum(first + k, found - 1)] >> 4) & 255
            gathered[at] += results[k]
        return 0

    lax.fori_loop(0, (found + AT_ONCE - 1) // AT_ONCE, several, 0)


def result_kernel(
    tops, gathered, fields, choose_top, couple_top, basis, up_leaf, up_pair, emission, reflect, out
):
    bands, rows, cols, leaf = out.shape
    leaves = rows * cols
    picks = couple_top.shape[1] // RANK
    leaf_field = fields[: bands * leaves, :RANK]
    pair_field = fields[bands * leaves :, :RANK]
    top_pick = dot(choose_top[...], tops[...], NN)
    top_pick = jnp.concatenate([top_pick] * (picks // 2), axis=1)
    kept = row_of(top_pick.shape, picks) == lax.broadcasted_iota(jnp.int32, top_pick.shape, 1) // RANK
    top_pick = jnp.where(kept, top_pick, 0.0).astype(BF16)
    top_field = dot(top_pick, couple_top[...], NT)
    top_field = jnp.sum(top_field.reshape(bands, picks, RANK), axis=1)
    spread = jnp.broadcast_to(top_field[:, None, :], (bands, cols, RANK))
    spread = spread.reshape(bands * cols, RANK).astype(BF16)
    pair_total = pair_field + own_blocks(dot(spread, up_pair[...], NT), cols)[:, :RANK]
    spread = jnp.broadcast_to(
        pair_total.reshape(bands, 1, cols, RANK), (bands, rows, cols, RANK)
    )
    spread = spread.reshape(bands * leaves, RANK).astype(BF16)
    leaf_total = leaf_field + own_blocks(dot(spread, up_leaf[...], NT), leaves)[:, :RANK]
    leaf_total = jnp.concatenate([leaf_total, leaf_total], axis=1)
    far_part = dot(on_diagonal(leaf_total, leaves), basis[...], NN)
    far_part = far_part.reshape(out.shape)
    for g in range(rows):
        near_part = jnp.swapaxes(gathered[g * cols : (g + 1) * cols], 0, 1)
        out[:, g] = emission[:, g] + reflect[:, g] * (near_part + far_part[:, g])


def body(
    radiosity,
    emission,
    reflect,
    basis,
    up_leaf,
    upward_pair_transfer,
    near_block,
    couple_leaf,
    couple_pair,
    couple_top,
    near_list,
    far_leaf,
    far_pair,
    far_top,
):
    around = lax.axis_size("perim")
    tall = lax.axis_size("section")
    bands, rows, cols, leaf = radiosity.shape
    leaves = rows * cols
    mates = [(s, s ^ 1) for s in range(tall)]
    others = [(s, s + 1 if s % 2 else s - 1) for s in range(1, tall - 1)]
    sems = pltpu.SemaphoreType.DMA
    basis = basis.reshape(leaves * RANK, leaf)
    up_leaf = up_leaf.reshape(leaves * RANK, RANK)
    up_pair = upward_pair_transfer.reshape(cols * RANK, RANK)
    sent, cells = pl.pallas_call(
        coefficients_kernel,
        out_shape=[
            pltpu.HBM((around, 16, WIDE), BF16),
            jax.ShapeDtypeStruct((leaves, bands, leaf), BF16),
        ],
        in_specs=[HBM] * 4,
        out_specs=[HBM, VMEM],
        scratch_shapes=[
            pltpu.VMEM(radiosity.shape, F32),
            pltpu.VMEM(basis.shape, BF16),
            pltpu.VMEM(up_leaf.shape, BF16),
            pltpu.VMEM(up_pair.shape, BF16),
            pltpu.VMEM((2, 16, WIDE), BF16),
            sems((around + 4,)),
        ],
        compiler_params=limit(4),
        name="coefficients",
    )(*map(far, [radiosity, basis, up_leaf, up_pair]))
    ring = lax.all_to_all(sent, "perim", 0, 0)
    blocks = near_block.reshape((leaves,) + near_block.shape[2:])
    couple_leaf = couple_leaf.reshape(leaves * RANK, -1)
    couple_pair = couple_pair.reshape(cols * RANK, -1)
    couple_top = couple_top[0, 0]
    listed = near_list.transpose(2, 0, 1)
    names_leaf = far_leaf.reshape(leaves, -1)
    names_pair = far_pair.reshape(cols, -1)
    names_top = far_top.reshape(1, -1)
    names = [names_leaf, names_pair, names_top]
    window = ((rows + 2) * (cols + 2), bands, leaf)
    choices = [
        pltpu.HBM((names_leaf.size, 3 * around * leaves), BF16),
        pltpu.HBM((names_pair.size, 3 * around * cols), BF16),
        pltpu.HBM((bands * names_top.size, tall * around * bands), BF16),
        pltpu.HBM((1, LANES), jnp.int32),
        jax.ShapeDtypeStruct((leaves, bands, leaf), F32),
    ]
    choose_leaf, choose_pair, choose_top, todo, local_part = pl.pallas_call(
        local_kernel,
        out_shape=choices,
        in_specs=[VMEM] + [HBM] * 5,
        out_specs=[HBM] * 4 + [VMEM],
        scratch_shapes=[
            pltpu.VMEM(window, F32),
            pltpu.SMEM(listed.shape, jnp.int32),
            pltpu.SMEM((1, LANES), jnp.int32),
        ]
        + [pltpu.VMEM(x.shape, x.dtype) for x in names + [blocks] + choices[:3]]
        + [sems((leaves + 9,))],
        compiler_params=limit(17),
        name="local",
    )(cells, *map(far, [listed] + names + [blocks]))
    packed = pl.pallas_call(
        packing_kernel,
        out_shape=jax.ShapeDtypeStruct((around * (leaves + cols) + leaves * 4 + 16, 512), BF16),
        in_specs=[VMEM, VMEM, ANY],
        out_specs=VMEM,
        compiler_params=limit(4),
        name="packing",
    )(ring, cells, local_part)
    tops = pl.pallas_call(
        tops_kernel,
        out_shape=pltpu.HBM((tall, around * bands, LANES), BF16),
        in_specs=[VMEM],
        out_specs=HBM,
        scratch_shapes=[pltpu.VMEM((around * bands, LANES), BF16), sems((tall,))],
        compiler_params=limit(3),
        name="tops",
    )(ring)
    from_mate = lax.ppermute(packed, "section", mates)
    from_other = lax.ppermute(packed, "section", others)
    tops = lax.all_to_all(tops, "section", 0, 0)
    most = leaves * (listed.shape[0] - 1)
    held = [choose_leaf, choose_pair, couple_leaf, couple_pair]
    gathered, fields = pl.pallas_call(
        field_kernel,
        out_shape=[
            jax.ShapeDtypeStruct((leaves, bands, leaf), F32),
            jax.ShapeDtypeStruct((bands * (leaves + cols), LANES), F32),
        ],
        in_specs=[VMEM] * 4 + [HBM] * 6,
        out_specs=[VMEM] * 2,
        scratch_shapes=[
            pltpu.VMEM((window[0] + 1,) + window[1:], F32),
            pltpu.SMEM(todo.shape, jnp.int32),
        ]
        + [pltpu.VMEM(x.shape, x.dtype) for x in held]
        + [pltpu.VMEM((most, leaf, leaf), BF16), sems((5,)), sems((most,))],
        compiler_params=limit(19),
        name="fields",
    )(
        packed,
        from_mate,
        from_other,
        local_part,
        *map(far, [todo] + held + [blocks]),
    )
    return pl.pallas_call(
        result_kernel,
        out_shape=jax.ShapeDtypeStruct(radiosity.shape, F32),
        in_specs=[VMEM] * 10,
        out_specs=VMEM,
        compiler_params=limit(4),
        name="result",
    )(
        tops.reshape(tall * around * bands, LANES),
        gathered,
        fields,
        choose_top,
        couple_top,
        basis,
        up_leaf,
        up_pair,
        emission,
        reflect,
    )


def solution(mesh):
    cells = P(None, "section", "perim", None)
    four = P("section", "perim", None, None)
    lists = P("section", "perim", None)
    return jax.shard_map(
        body,
        mesh=mesh,
        in_specs=(cells,) * 3
        + (four,) * 3
        + (P("section", "perim", None, None, None),)
        + (four,) * 3
        + (lists,) * 4,
        out_specs=cells,
        check_vma=False,
    )
```

```python
import jax
import jax.numpy as jnp
from jax import lax
from jax.experimental import pallas as pl
from jax.experimental.pallas import tpu as pltpu
from jax.sharding import PartitionSpec as P

F32 = jnp.float32
BF16 = jnp.bfloat16
NT = (((1,), (1,)), ((), ()))
NN = (((1,), (0,)), ((), ()))
LANES = 128
RANK = 64
WIDE = 1152
VMEM = pl.BlockSpec(memory_space=pltpu.VMEM)
HBM = pl.BlockSpec(memory_space=pltpu.HBM)
ANY = pl.BlockSpec(memory_space=pl.ANY)
AT_ONCE = 16


def dot(left, right, dims):
    return lax.dot_general(left, right, dims, preferred_element_type=F32)


def far(x):
    return pltpu.with_memory_space_constraint(x, pltpu.HBM)


def limit(mib):
    return pltpu.CompilerParams(vmem_limit_bytes=mib * 1024 * 1024)


def row_of(shape, count):
    return lax.broadcasted_iota(jnp.int32, shape, 0) % count


def own_blocks(products, count):
    shape = (products.shape[0], LANES)
    mine = row_of(shape, count) - lax.broadcasted_iota(jnp.int32, shape, 1) // RANK
    total = jnp.zeros(shape, F32)
    for tile in range(count // 2):
        total += jnp.where(mine == 2 * tile, products[:, tile * LANES : (tile + 1) * LANES], 0.0)
    return total + pltpu.roll(total, RANK, 1)


def on_diagonal(twice, count):
    mine = row_of(twice.shape, count) - lax.broadcasted_iota(jnp.int32, twice.shape, 1) // RANK
    tiles = [jnp.where(mine == 2 * tile, twice, 0.0) for tile in range(count // 2)]
    return jnp.concatenate(tiles, axis=1).astype(BF16)


def side_by_side(twice, count):
    low = lax.broadcasted_iota(jnp.int32, (count, LANES), 1) < RANK
    return jnp.concatenate(
        [
            jnp.where(low, twice[b * count : (b + 1) * count], twice[(b + 1) * count : (b + 2) * count])
            for b in range(0, twice.shape[0] // count, 2)
        ],
        axis=1,
    )


def started(copies, sems, at=0):
    made = []
    for number, (source, target) in enumerate(copies):
        made.append(pltpu.make_async_copy(source, target, sems.at[at + number]))
        made[-1].start()
    return made


def coefficients_kernel(
    far_radiosity,
    far_basis,
    far_up_leaf,
    far_up_pair,
    sent,
    cells,
    radiosity,
    basis,
    up_leaf,
    up_pair,
    block,
    sems,
):
    copies = started(
        [
            (far_radiosity, radiosity),
            (far_basis, basis),
            (far_up_leaf, up_leaf),
            (far_up_pair, up_pair),
        ],
        sems,
    )
    copies[0].wait()
    column = lax.axis_index("perim")
    bands, rows, cols, leaf = radiosity.shape
    leaves = rows * cols
    shaded = radiosity[...].reshape(bands * leaves, leaf).astype(BF16)
    copies[1].wait()
    leaf_twice = own_blocks(dot(shaded, basis[...], NT), leaves)
    of_pairs = leaf_twice.reshape(bands, rows, cols, LANES)
    of_pairs = jnp.concatenate(
        [on_diagonal(of_pairs[:, g].reshape(bands * cols, LANES), cols) for g in range(rows)],
        axis=1,
    )
    copies[2].wait()
    pair = dot(of_pairs, up_leaf[...], NN)
    pair_twice = jnp.concatenate([pair, pair], axis=1)
    copies[3].wait()
    top = dot(on_diagonal(pair_twice, cols), up_pair[...], NN)
    top = jnp.sum(top.reshape(bands, cols, RANK), axis=1)
    top_twice = jnp.concatenate([top, top], axis=1)

    def edge(col):
        return jnp.concatenate(
            [radiosity[:, g, col, :] for g in range(rows)], axis=1
        )

    leaf_part = side_by_side(leaf_twice, leaves)
    pair_part = side_by_side(pair_twice, cols)
    top_part = jnp.concatenate([top_twice, jnp.zeros_like(top_twice)], axis=0)

    for right, col in enumerate((0, cols - 1)):
        block[right] = jnp.concatenate(
            [leaf_part, jnp.concatenate([pair_part, edge(col)], axis=0), top_part], axis=1
        ).astype(BF16)
    around = sent.shape[0]
    to_right = (column + 1) % around
    copies = started(
        [(block.at[jnp.where(to_right == to, 1, 0)], sent.at[to]) for to in range(around)], sems, 4
    )
    for g in range(rows):
        turned = jnp.swapaxes(radiosity[:, g], 0, 1)
        cells[g * cols : (g + 1) * cols] = turned.astype(BF16)
    for copy in copies:
        copy.wait()


def packing_kernel(ring, cells, local_part, packed):
    column = lax.axis_index("perim")
    around, leaves = ring.shape[:2]
    cols = leaves // 2
    for at in range(around):
        packed[at * leaves : (at + 1) * leaves] = ring[at, :, :512]
    for at in range(0, around, 2):
        start = around * leaves + at * cols
        both = [ring[at + k, :, 512:1024].astype(F32)[:cols] for k in range(2)]
        packed[start : start + 2 * cols] = jnp.concatenate(both, axis=0).astype(BF16)
    start = around * (leaves + cols)
    for at in range(0, leaves, 4):
        four = [cells[at + k].astype(F32) for k in range(4)]
        two = [jnp.concatenate(four[:2], axis=1), jnp.concatenate(four[2:], axis=1)]
        packed[start + at * 4 : start + at * 4 + 16] = jnp.concatenate(two, axis=0).astype(BF16)
    start += leaves * 4
    sides = [(column + around - 1) % around, (column + 1) % around]
    both = [ring[at, :, 512:1024].astype(F32)[8:] for at in sides]
    packed[start : start + 16] = jnp.concatenate(both, axis=0).astype(BF16)


def tops_kernel(ring, tops, row_tops, sems):
    rows = ring[:, :, 1024:].astype(F32)[:, :8]
    half = rows.shape[0] // 2
    low = lax.broadcasted_iota(jnp.int32, rows[:half].shape, 2) < RANK
    rows = jnp.where(low, rows[:half], rows[half:])
    row_tops[...] = rows.reshape(row_tops.shape).astype(BF16)
    for copy in started([(row_tops, tops.at[to]) for to in range(tops.shape[0])], sems):
        copy.wait()


def one_hot(tier, inner, size):
    count, picks = inner.shape
    slots = tier * size + inner
    at = lax.broadcasted_iota(jnp.int32, (count, 3 * size), 1)
    return jnp.concatenate(
        [(at == slots[:, k : k + 1]).astype(F32) for k in range(picks)], axis=0
    ).astype(BF16)


def near_products(seen, blocks):
    total = jnp.zeros(seen[0].shape, F32)
    turned = jnp.zeros(seen[0].shape[::-1], F32)
    for n, cell in enumerate(seen):
        if n % 2 == 0:
            total += dot(cell, blocks[n], NT)
        else:
            turned += dot(blocks[n], cell, NT)
    return total + turned.T


def split_name(name, width_all):
    if width_all & (width_all - 1):
        return name // width_all, name % width_all
    return name >> (width_all.bit_length() - 1), name & (width_all - 1)


def position(name, section, column, rows, cols, width_all):
    row = split_name(name, width_all)[0]
    turn = split_name(name + (width_all + 1 - cols * column), width_all)[1]
    return row - (rows * section - 1), turn


def local_kernel(
    cells,
    far_listed,
    far_names_leaf,
    far_names_pair,
    far_names_top,
    far_blocks,
    far_choose_leaf,
    far_choose_pair,
    far_choose_top,
    far_todo,
    local_part,
    window,
    listed,
    todo,
    names_leaf,
    names_pair,
    names_top,
    blocks,
    choose_leaf,
    choose_pair,
    choose_top,
    sems,
):
    leaves, count = blocks.shape[:2]
    lists = started(
        [
            (far_names_leaf, names_leaf),
            (far_names_pair, names_pair),
            (far_names_top, names_top),
            (far_listed, listed),
        ],
        sems,
    )
    block_copies = started(
        [(far_blocks.at[at], blocks.at[at]) for at in range(leaves)], sems, len(lists)
    )
    for copy in lists:
        copy.wait()
    section, column = lax.axis_index("section"), lax.axis_index("perim")
    cols = names_pair.shape[0]
    rows = leaves // cols
    width_all = choose_pair.shape[1] // 3
    mate = section + 1 - 2 * (section % 2)

    def tier_of(source):
        return jnp.where(source == section, 0, jnp.where(source == mate, 1, 2))

    names = names_leaf[...]
    height, turn = split_name(names, width_all)
    source, height = split_name(height, rows)
    device, turn = split_name(turn, cols)
    choose_leaf[...] = one_hot(
        tier_of(source), device * leaves + height * cols + turn, width_all * rows
    )
    height, turn = split_name(names_pair[...], width_all)
    choose_pair[...] = one_hot(tier_of(height), turn, width_all)
    picks = names_top.shape[1]
    bands = choose_top.shape[0] // picks
    square = (picks, picks)
    names = jnp.broadcast_to(names_top[...], square)
    diagonal = lax.broadcasted_iota(jnp.int32, square, 0) == lax.broadcasted_iota(jnp.int32, square, 1)
    names = jnp.sum(jnp.where(diagonal, names, 0), axis=1, keepdims=True)
    around = width_all // cols
    row, source = split_name(names, around)
    upper, source = split_name(source, around // 2)
    names = upper * (choose_top.shape[1] // bands // 2) + row * (around // 2) + source
    at = lax.broadcasted_iota(jnp.int32, (picks, choose_top.shape[1]), 1)
    choose_top[...] = jnp.concatenate(
        [(at == names * bands + b).astype(F32) for b in range(bands)], axis=0
    ).astype(BF16)
    results = started(
        [
            (choose_leaf, far_choose_leaf),
            (choose_pair, far_choose_pair),
            (choose_top, far_choose_top),
        ],
        sems,
        len(lists) + leaves,
    )
    broad = cols + 2
    window[...] = jnp.zeros_like(window)
    for g in range(rows):
        start = (g + 1) * broad + 1
        window[start : start + cols] = cells[g * cols : (g + 1) * cols].astype(F32)
    found = jnp.int32(0)
    for at in range(leaves):
        seen = []
        for n in range(count):
            name = listed[n, at // cols, at % cols]
            up, turn = position(name, section, column, rows, cols, width_all)
            where = up * broad + turn
            seen.append(window[where].astype(BF16))
            if n > 0:
                todo[0, found] = (where << 12) + (at << 4) + n
                inside = (up >= 1) & (up <= rows) & (turn >= 1) & (turn <= cols)
                found = found + jnp.where(inside, 0, 1)
        if at % 2 == 0:
            for copy in block_copies[at : at + 2]:
                copy.wait()
        local_part[at] = near_products(seen, blocks.at[at])
    todo[0, todo.shape[1] - 1] = found
    results += started(
        [(todo, far_todo)], sems, len(lists) + leaves + 3
    )
    for copy in results:
        copy.wait()


def chosen(choose, tables, start, count):
    size = choose.shape[1] // 3
    picks = choose.shape[0] // count
    result = jnp.zeros((count * picks, 512), F32)
    for number, table in enumerate(tables):
        result += dot(
            choose[:, number * size : (number + 1) * size], table[start : start + size], NN
        )
    low = lax.broadcasted_iota(jnp.int32, (count, LANES), 1) < RANK
    bands = []
    for n in range(4):
        even, odd = [], []
        for k in range(0, picks, 2):
            one = result[k * count : (k + 1) * count, n * LANES : (n + 1) * LANES]
            two = result[(k + 1) * count : (k + 2) * count, n * LANES : (n + 1) * LANES]
            even.append(jnp.where(low, one, pltpu.roll(two, RANK, 1)))
            odd.append(jnp.where(low, pltpu.roll(one, RANK, 1), two))
        bands += [jnp.concatenate(even, axis=1), jnp.concatenate(odd, axis=1)]
    return jnp.concatenate(bands, axis=0).astype(BF16)


def field_kernel(
    own,
    from_mate,
    from_other,
    local_part,
    far_todo,
    far_choose_leaf,
    far_choose_pair,
    far_couple_leaf,
    far_couple_pair,
    far_blocks,
    gathered,
    fields,
    window,
    todo,
    choose_leaf,
    choose_pair,
    couple_leaf,
    couple_pair,
    blocks,
    sems,
    block_sems,
):
    copies = started(
        [
            (far_todo, todo),
            (far_choose_leaf, choose_leaf),
            (far_choose_pair, choose_pair),
            (far_couple_leaf, couple_leaf),
            (far_couple_pair, couple_pair),
        ],
        sems,
    )
    leaves = gathered.shape[0]
    section = lax.axis_index("section")
    bands, leaf = gathered.shape[1:]
    cols = fields.shape[0] // bands - leaves
    rows = leaves // cols
    around = (own.shape[0] - 16 - leaves * 4) // (leaves + cols)
    broad = cols + 2
    width_all = around * cols
    odd = section % 2
    cells_at = around * (leaves + cols)
    sides_at = cells_at + leaves * 4

    def seen_row(source, g, at):
        for p in range(0, cols, 4):
            start = cells_at + (g * cols + p) * 4
            four = source[start : start + 16].astype(F32)
            for k in range(4):
                lanes = slice(k % 2 * leaf, (k % 2 + 1) * leaf)
                window[at * broad + 1 + p + k] = four[k // 2 * 8 : (k // 2 + 1) * 8, lanes]
        two = source[sides_at : sides_at + 16].astype(F32)[:, g * leaf : (g + 1) * leaf]
        window[at * broad] = two[:8]
        window[(at + 1) * broad - 1] = two[8:]

    for g in range(rows):
        seen_row(own, g, g + 1)

    @pl.when(odd == 0)
    def _():
        seen_row(from_other, rows - 1, 0)
        seen_row(from_mate, 0, rows + 1)

    @pl.when(odd == 1)
    def _():
        seen_row(from_mate, rows - 1, 0)
        seen_row(from_other, 0, rows + 1)

    zero_cell = window.shape[0] - 1
    window[zero_cell] = jnp.zeros(window.shape[1:], F32)
    copies[0].wait()

    found = todo[0, todo.shape[1] - 1]

    def block_copy(at, n, slot):
        return pltpu.make_async_copy(
            far_blocks.at[at, n], blocks.at[slot], block_sems.at[slot]
        )

    def fetch(step, _):
        for k in range(4):
            slot = 4 * step + k

            @pl.when(slot < found)
            def _():
                pair = todo[0, slot]
                block_copy((pair >> 4) & 255, pair & 15, slot).start()

        return 0

    lax.fori_loop(0, (found + 3) // 4, fetch, 0)
    tables = (own, from_mate, from_other)
    copies[1].wait()
    leaf_pick = chosen(choose_leaf, tables, 0, leaves)
    copies[2].wait()
    pair_pick = chosen(choose_pair, tables, around * leaves, cols)
    split = bands * leaves
    copies[3].wait()
    fields[:split] = own_blocks(dot(leaf_pick, couple_leaf[...], NT), leaves)
    copies[4].wait()
    fields[split:] = own_blocks(dot(pair_pick, couple_pair[...], NT), cols)
    gathered[...] = local_part[...]

    def several(step, _):
        first = step * AT_ONCE
        for k in range(AT_ONCE):

            @pl.when(first + k < found)
            def _():
                block_copy(0, 0, first + k).wait()

        results = []
        for k in range(AT_ONCE):
            slot = jnp.minimum(first + k, found - 1)
            where = jnp.where(first + k < found, todo[0, slot] >> 12, zero_cell)
            cell = window[where].astype(BF16)
            if k % 2 == 0:
                results.append(dot(cell, blocks[slot], NT))
            else:
                results.append(dot(blocks[slot], cell, NT).T)
        for k in range(AT_ONCE):
            at = (todo[0, jnp.minimum(first + k, found - 1)] >> 4) & 255
            gathered[at] += results[k]
        return 0

    lax.fori_loop(0, (found + AT_ONCE - 1) // AT_ONCE, several, 0)


def result_kernel(
    tops, gathered, fields, choose_top, couple_top, basis, up_leaf, up_pair, emission, reflect, out
):
    bands, rows, cols, leaf = out.shape
    leaves = rows * cols
    picks = couple_top.shape[1] // RANK
    leaf_field = fields[: bands * leaves, :RANK]
    pair_field = fields[bands * leaves :, :RANK]
    size = tops.shape[0]
    top_pick = dot(choose_top[:, :size], tops[...], NN)
    upper = dot(choose_top[:, size:], tops[...], NN)
    top_pick = jnp.where(lax.broadcasted_iota(jnp.int32, upper.shape, 1) < RANK, top_pick, upper)
    top_pick = top_pick + pltpu.roll(top_pick, RANK, 1)
    top_pick = jnp.concatenate([top_pick] * (picks // 2), axis=1)
    kept = row_of(top_pick.shape, picks) == lax.broadcasted_iota(jnp.int32, top_pick.shape, 1) // RANK
    top_pick = jnp.where(kept, top_pick, 0.0).astype(BF16)
    top_field = dot(top_pick, couple_top[...], NT)
    top_field = jnp.sum(top_field.reshape(bands, picks, RANK), axis=1)
    spread = jnp.broadcast_to(top_field[:, None, :], (bands, cols, RANK))
    spread = spread.reshape(bands * cols, RANK).astype(BF16)
    pair_total = pair_field + own_blocks(dot(spread, up_pair[...], NT), cols)[:, :RANK]
    spread = jnp.broadcast_to(
        pair_total.reshape(bands, 1, cols, RANK), (bands, rows, cols, RANK)
    )
    spread = spread.reshape(bands * leaves, RANK).astype(BF16)
    leaf_total = leaf_field + own_blocks(dot(spread, up_leaf[...], NT), leaves)[:, :RANK]
    leaf_total = jnp.concatenate([leaf_total, leaf_total], axis=1)
    far_part = dot(on_diagonal(leaf_total, leaves), basis[...], NN)
    far_part = far_part.reshape(out.shape)
    for g in range(rows):
        near_part = jnp.swapaxes(gathered[g * cols : (g + 1) * cols], 0, 1)
        out[:, g] = emission[:, g] + reflect[:, g] * (near_part + far_part[:, g])


def body(
    radiosity,
    emission,
    reflect,
    basis,
    up_leaf,
    upward_pair_transfer,
    near_block,
    couple_leaf,
    couple_pair,
    couple_top,
    near_list,
    far_leaf,
    far_pair,
    far_top,
):
    around = lax.axis_size("perim")
    tall = lax.axis_size("section")
    bands, rows, cols, leaf = radiosity.shape
    leaves = rows * cols
    mates = [(s, s ^ 1) for s in range(tall)]
    others = [(s, s + 1 if s % 2 else s - 1) for s in range(1, tall - 1)]
    sems = pltpu.SemaphoreType.DMA
    basis = basis.reshape(leaves * RANK, leaf)
    up_leaf = up_leaf.reshape(leaves * RANK, RANK)
    up_pair = upward_pair_transfer.reshape(cols * RANK, RANK)
    sent, cells = pl.pallas_call(
        coefficients_kernel,
        out_shape=[
            pltpu.HBM((around, 16, WIDE), BF16),
            jax.ShapeDtypeStruct((leaves, bands, leaf), BF16),
        ],
        in_specs=[HBM] * 4,
        out_specs=[HBM, VMEM],
        scratch_shapes=[
            pltpu.VMEM(radiosity.shape, F32),
            pltpu.VMEM(basis.shape, BF16),
            pltpu.VMEM(up_leaf.shape, BF16),
            pltpu.VMEM(up_pair.shape, BF16),
            pltpu.VMEM((2, 16, WIDE), BF16),
            sems((around + 4,)),
        ],
        compiler_params=limit(4),
        name="coefficients",
    )(*map(far, [radiosity, basis, up_leaf, up_pair]))
    ring = lax.all_to_all(sent, "perim", 0, 0)
    blocks = near_block.reshape((leaves,) + near_block.shape[2:])
    couple_leaf = couple_leaf.reshape(leaves * RANK, -1)
    couple_pair = couple_pair.reshape(cols * RANK, -1)
    couple_top = couple_top[0, 0]
    listed = near_list.transpose(2, 0, 1)
    names_leaf = far_leaf.reshape(leaves, -1)
    names_pair = far_pair.reshape(cols, -1)
    names_top = far_top.reshape(1, -1)
    names = [names_leaf, names_pair, names_top]
    window = ((rows + 2) * (cols + 2), bands, leaf)
    choices = [
        pltpu.HBM((names_leaf.size, 3 * around * leaves), BF16),
        pltpu.HBM((names_pair.size, 3 * around * cols), BF16),
        pltpu.HBM((bands * names_top.size, tall * around * bands), BF16),
        pltpu.HBM((1, LANES), jnp.int32),
        jax.ShapeDtypeStruct((leaves, bands, leaf), F32),
    ]
    choose_leaf, choose_pair, choose_top, todo, local_part = pl.pallas_call(
        local_kernel,
        out_shape=choices,
        in_specs=[VMEM] + [HBM] * 5,
        out_specs=[HBM] * 4 + [VMEM],
        scratch_shapes=[
            pltpu.VMEM(window, F32),
            pltpu.SMEM(listed.shape, jnp.int32),
            pltpu.SMEM((1, LANES), jnp.int32),
        ]
        + [pltpu.VMEM(x.shape, x.dtype) for x in names + [blocks] + choices[:3]]
        + [sems((leaves + 9,))],
        compiler_params=limit(17),
        name="local",
    )(cells, *map(far, [listed] + names + [blocks]))
    packed = pl.pallas_call(
        packing_kernel,
        out_shape=jax.ShapeDtypeStruct((around * (leaves + cols) + leaves * 4 + 16, 512), BF16),
        in_specs=[VMEM, VMEM, ANY],
        out_specs=VMEM,
        compiler_params=limit(4),
        name="packing",
    )(ring, cells, local_part)
    tops = pl.pallas_call(
        tops_kernel,
        out_shape=pltpu.HBM((tall, around * bands // 2, LANES), BF16),
        in_specs=[VMEM],
        out_specs=HBM,
        scratch_shapes=[pltpu.VMEM((around * bands // 2, LANES), BF16), sems((tall,))],
        compiler_params=limit(3),
        name="tops",
    )(ring)
    from_mate = lax.ppermute(packed, "section", mates)
    from_other = lax.ppermute(packed, "section", others)
    tops = lax.all_to_all(tops, "section", 0, 0)
    most = leaves * (listed.shape[0] - 1)
    held = [choose_leaf, choose_pair, couple_leaf, couple_pair]
    gathered, fields = pl.pallas_call(
        field_kernel,
        out_shape=[
            jax.ShapeDtypeStruct((leaves, bands, leaf), F32),
            jax.ShapeDtypeStruct((bands * (leaves + cols), LANES), F32),
        ],
        in_specs=[VMEM] * 4 + [HBM] * 6,
        out_specs=[VMEM] * 2,
        scratch_shapes=[
            pltpu.VMEM((window[0] + 1,) + window[1:], F32),
            pltpu.SMEM(todo.shape, jnp.int32),
        ]
        + [pltpu.VMEM(x.shape, x.dtype) for x in held]
        + [pltpu.VMEM((most, leaf, leaf), BF16), sems((5,)), sems((most,))],
        compiler_params=limit(19),
        name="fields",
    )(
        packed,
        from_mate,
        from_other,
        local_part,
        *map(far, [todo] + held + [blocks]),
    )
    return pl.pallas_call(
        result_kernel,
        out_shape=jax.ShapeDtypeStruct(radiosity.shape, F32),
        in_specs=[VMEM] * 10,
        out_specs=VMEM,
        compiler_params=limit(4),
        name="result",
    )(
        tops.reshape(tall * around * bands // 2, LANES),
        gathered,
        fields,
        choose_top,
        couple_top,
        basis,
        up_leaf,
        up_pair,
        emission,
        reflect,
    )


def solution(mesh):
    cells = P(None, "section", "perim", None)
    four = P("section", "perim", None, None)
    lists = P("section", "perim", None)
    return jax.shard_map(
        body,
        mesh=mesh,
        in_specs=(cells,) * 3
        + (four,) * 3
        + (P("section", "perim", None, None, None),)
        + (four,) * 3
        + (lists,) * 4,
        out_specs=cells,
        check_vma=False,
    )
```

```python
import jax
import jax.numpy as jnp
from jax import lax
from jax.experimental import pallas as pl
from jax.experimental.pallas import tpu as pltpu
from jax.sharding import PartitionSpec as P

F32 = jnp.float32
BF16 = jnp.bfloat16
NT = (((1,), (1,)), ((), ()))
NN = (((1,), (0,)), ((), ()))
LANES = 128
RANK = 64
WIDE = 1152
VMEM = pl.BlockSpec(memory_space=pltpu.VMEM)
HBM = pl.BlockSpec(memory_space=pltpu.HBM)
ANY = pl.BlockSpec(memory_space=pl.ANY)
AT_ONCE = 20


def dot(left, right, dims):
    return lax.dot_general(left, right, dims, preferred_element_type=F32)


def far(x):
    return pltpu.with_memory_space_constraint(x, pltpu.HBM)


def limit(mib):
    return pltpu.CompilerParams(vmem_limit_bytes=mib * 1024 * 1024)


def row_of(shape, count):
    return lax.broadcasted_iota(jnp.int32, shape, 0) % count


def own_blocks(products, count):
    shape = (products.shape[0], LANES)
    mine = row_of(shape, count) - lax.broadcasted_iota(jnp.int32, shape, 1) // RANK
    total = jnp.zeros(shape, F32)
    for tile in range(count // 2):
        total += jnp.where(mine == 2 * tile, products[:, tile * LANES : (tile + 1) * LANES], 0.0)
    return total + pltpu.roll(total, RANK, 1)


def on_diagonal(twice, count):
    mine = row_of(twice.shape, count) - lax.broadcasted_iota(jnp.int32, twice.shape, 1) // RANK
    tiles = [jnp.where(mine == 2 * tile, twice, 0.0) for tile in range(count // 2)]
    return jnp.concatenate(tiles, axis=1).astype(BF16)


def side_by_side(twice, count):
    low = lax.broadcasted_iota(jnp.int32, (count, LANES), 1) < RANK
    return jnp.concatenate(
        [
            jnp.where(low, twice[b * count : (b + 1) * count], twice[(b + 1) * count : (b + 2) * count])
            for b in range(0, twice.shape[0] // count, 2)
        ],
        axis=1,
    )


def started(copies, sems, at=0):
    made = []
    for number, (source, target) in enumerate(copies):
        made.append(pltpu.make_async_copy(source, target, sems.at[at + number]))
        made[-1].start()
    return made


def coefficients_kernel(
    far_radiosity,
    far_basis,
    far_up_leaf,
    far_up_pair,
    sent,
    cells,
    radiosity,
    basis,
    up_leaf,
    up_pair,
    block,
    sems,
):
    copies = started(
        [
            (far_radiosity, radiosity),
            (far_basis, basis),
            (far_up_leaf, up_leaf),
            (far_up_pair, up_pair),
        ],
        sems,
    )
    copies[0].wait()
    column = lax.axis_index("perim")
    bands, rows, cols, leaf = radiosity.shape
    leaves = rows * cols
    shaded = radiosity[...].reshape(bands * leaves, leaf).astype(BF16)
    copies[1].wait()
    leaf_twice = own_blocks(dot(shaded, basis[...], NT), leaves)
    of_pairs = leaf_twice.reshape(bands, rows, cols, LANES)
    of_pairs = jnp.concatenate(
        [on_diagonal(of_pairs[:, g].reshape(bands * cols, LANES), cols) for g in range(rows)],
        axis=1,
    )
    copies[2].wait()
    pair = dot(of_pairs, up_leaf[...], NN)
    pair_twice = jnp.concatenate([pair, pair], axis=1)
    copies[3].wait()
    top = dot(on_diagonal(pair_twice, cols), up_pair[...], NN)
    top = jnp.sum(top.reshape(bands, cols, RANK), axis=1)
    top_twice = jnp.concatenate([top, top], axis=1)

    def edge(col):
        return jnp.concatenate(
            [radiosity[:, g, col, :] for g in range(rows)], axis=1
        )

    leaf_part = side_by_side(leaf_twice, leaves)
    pair_part = side_by_side(pair_twice, cols)
    top_part = jnp.concatenate([top_twice, jnp.zeros_like(top_twice)], axis=0)

    for right, col in enumerate((0, cols - 1)):
        block[right] = jnp.concatenate(
            [leaf_part, jnp.concatenate([pair_part, edge(col)], axis=0), top_part], axis=1
        ).astype(BF16)
    around = sent.shape[0]
    to_right = (column + 1) % around
    copies = started(
        [(block.at[jnp.where(to_right == to, 1, 0)], sent.at[to]) for to in range(around)], sems, 4
    )
    for g in range(rows):
        turned = jnp.swapaxes(radiosity[:, g], 0, 1)
        cells[g * cols : (g + 1) * cols] = turned.astype(BF16)
    for copy in copies:
        copy.wait()


def packing_kernel(ring, cells, local_part, packed):
    column = lax.axis_index("perim")
    around, leaves = ring.shape[:2]
    cols = leaves // 2
    for at in range(around):
        packed[at * leaves : (at + 1) * leaves] = ring[at, :, :512]
    for at in range(0, around, 2):
        start = around * leaves + at * cols
        both = [ring[at + k, :, 512:1024].astype(F32)[:cols] for k in range(2)]
        packed[start : start + 2 * cols] = jnp.concatenate(both, axis=0).astype(BF16)
    start = around * (leaves + cols)
    for at in range(0, leaves, 4):
        four = [cells[at + k].astype(F32) for k in range(4)]
        two = [jnp.concatenate(four[:2], axis=1), jnp.concatenate(four[2:], axis=1)]
        packed[start + at * 4 : start + at * 4 + 16] = jnp.concatenate(two, axis=0).astype(BF16)
    start += leaves * 4
    sides = [(column + around - 1) % around, (column + 1) % around]
    both = [ring[at, :, 512:1024].astype(F32)[8:] for at in sides]
    packed[start : start + 16] = jnp.concatenate(both, axis=0).astype(BF16)


def tops_kernel(ring, tops, row_tops, sems):
    rows = ring[:, :, 1024:].astype(F32)[:, :8]
    half = rows.shape[0] // 2
    low = lax.broadcasted_iota(jnp.int32, rows[:half].shape, 2) < RANK
    rows = jnp.where(low, rows[:half], rows[half:])
    row_tops[...] = rows.reshape(row_tops.shape).astype(BF16)
    for copy in started([(row_tops, tops.at[to]) for to in range(tops.shape[0])], sems):
        copy.wait()


def one_hot(tier, inner, size):
    count, picks = inner.shape
    slots = tier * size + inner
    at = lax.broadcasted_iota(jnp.int32, (count, 3 * size), 1)
    return jnp.concatenate(
        [(at == slots[:, k : k + 1]).astype(F32) for k in range(picks)], axis=0
    ).astype(BF16)


def near_products(seen, blocks):
    total = jnp.zeros(seen[0].shape, F32)
    turned = jnp.zeros(seen[0].shape[::-1], F32)
    for n, cell in enumerate(seen):
        if n % 2 == 0:
            total += dot(cell, blocks[n], NT)
        else:
            turned += dot(blocks[n], cell, NT)
    return total + turned.T


def split_name(name, width_all):
    if width_all & (width_all - 1):
        return name // width_all, name % width_all
    return name >> (width_all.bit_length() - 1), name & (width_all - 1)


def position(name, section, column, rows, cols, width_all):
    row = split_name(name, width_all)[0]
    turn = split_name(name + (width_all + 1 - cols * column), width_all)[1]
    return row - (rows * section - 1), turn


def local_kernel(
    cells,
    far_listed,
    far_names_leaf,
    far_names_pair,
    far_names_top,
    far_blocks,
    far_choose_leaf,
    far_choose_pair,
    far_choose_top,
    far_todo,
    local_part,
    window,
    listed,
    todo,
    names_leaf,
    names_pair,
    names_top,
    blocks,
    choose_leaf,
    choose_pair,
    choose_top,
    sems,
):
    leaves, count = blocks.shape[:2]
    lists = started(
        [
            (far_names_leaf, names_leaf),
            (far_names_pair, names_pair),
            (far_names_top, names_top),
            (far_listed, listed),
        ],
        sems,
    )
    block_copies = started(
        [(far_blocks.at[at], blocks.at[at]) for at in range(leaves)], sems, len(lists)
    )
    for copy in lists:
        copy.wait()
    section, column = lax.axis_index("section"), lax.axis_index("perim")
    cols = names_pair.shape[0]
    rows = leaves // cols
    width_all = choose_pair.shape[1] // 3
    mate = section + 1 - 2 * (section % 2)

    def tier_of(source):
        return jnp.where(source == section, 0, jnp.where(source == mate, 1, 2))

    names = names_leaf[...]
    height, turn = split_name(names, width_all)
    source, height = split_name(height, rows)
    device, turn = split_name(turn, cols)
    choose_leaf[...] = one_hot(
        tier_of(source), device * leaves + height * cols + turn, width_all * rows
    )
    height, turn = split_name(names_pair[...], width_all)
    choose_pair[...] = one_hot(tier_of(height), turn, width_all)
    picks = names_top.shape[1]
    bands = choose_top.shape[0] // picks
    square = (picks, picks)
    names = jnp.broadcast_to(names_top[...], square)
    diagonal = lax.broadcasted_iota(jnp.int32, square, 0) == lax.broadcasted_iota(jnp.int32, square, 1)
    names = jnp.sum(jnp.where(diagonal, names, 0), axis=1, keepdims=True)
    around = width_all // cols
    row, source = split_name(names, around)
    upper, source = split_name(source, around // 2)
    names = upper * (choose_top.shape[1] // bands // 2) + row * (around // 2) + source
    at = lax.broadcasted_iota(jnp.int32, (picks, choose_top.shape[1]), 1)
    choose_top[...] = jnp.concatenate(
        [(at == names * bands + b).astype(F32) for b in range(bands)], axis=0
    ).astype(BF16)
    results = started(
        [
            (choose_leaf, far_choose_leaf),
            (choose_pair, far_choose_pair),
            (choose_top, far_choose_top),
        ],
        sems,
        len(lists) + leaves,
    )
    broad = cols + 2
    window[...] = jnp.zeros_like(window)
    for g in range(rows):
        start = (g + 1) * broad + 1
        window[start : start + cols] = cells[g * cols : (g + 1) * cols].astype(F32)
    found = jnp.int32(0)
    for at in range(leaves):
        seen = []
        for n in range(count):
            name = listed[n, at // cols, at % cols]
            up, turn = position(name, section, column, rows, cols, width_all)
            where = up * broad + turn
            seen.append(window[where].astype(BF16))
            if n > 0:
                todo[0, found] = (where << 12) + (at << 4) + n
                inside = (up >= 1) & (up <= rows) & (turn >= 1) & (turn <= cols)
                found = found + jnp.where(inside, 0, 1)
        if at % 2 == 0:
            for copy in block_copies[at : at + 2]:
                copy.wait()
        local_part[at] = near_products(seen, blocks.at[at])
    todo[0, todo.shape[1] - 1] = found
    results += started(
        [(todo, far_todo)], sems, len(lists) + leaves + 3
    )
    for copy in results:
        copy.wait()


def chosen(choose, tables, start, count):
    size = choose.shape[1] // 3
    picks = choose.shape[0] // count
    result = jnp.zeros((count * picks, 512), F32)
    for number, table in enumerate(tables):
        result += dot(
            choose[:, number * size : (number + 1) * size], table[start : start + size], NN
        )
    low = lax.broadcasted_iota(jnp.int32, (count, LANES), 1) < RANK
    bands = []
    for n in range(4):
        even, odd = [], []
        for k in range(0, picks, 2):
            one = result[k * count : (k + 1) * count, n * LANES : (n + 1) * LANES]
            two = result[(k + 1) * count : (k + 2) * count, n * LANES : (n + 1) * LANES]
            even.append(jnp.where(low, one, pltpu.roll(two, RANK, 1)))
            odd.append(jnp.where(low, pltpu.roll(one, RANK, 1), two))
        bands += [jnp.concatenate(even, axis=1), jnp.concatenate(odd, axis=1)]
    return jnp.concatenate(bands, axis=0).astype(BF16)


def field_kernel(
    own,
    from_mate,
    from_other,
    local_part,
    far_todo,
    far_choose_leaf,
    far_choose_pair,
    far_couple_leaf,
    far_couple_pair,
    far_blocks,
    gathered,
    fields,
    window,
    todo,
    choose_leaf,
    choose_pair,
    couple_leaf,
    couple_pair,
    blocks,
    sems,
    block_sems,
):
    copies = started(
        [
            (far_todo, todo),
            (far_choose_leaf, choose_leaf),
            (far_choose_pair, choose_pair),
            (far_couple_leaf, couple_leaf),
            (far_couple_pair, couple_pair),
        ],
        sems,
    )
    leaves = gathered.shape[0]
    section = lax.axis_index("section")
    bands, leaf = gathered.shape[1:]
    cols = fields.shape[0] // bands - leaves
    rows = leaves // cols
    around = (own.shape[0] - 16 - leaves * 4) // (leaves + cols)
    broad = cols + 2
    width_all = around * cols
    odd = section % 2
    cells_at = around * (leaves + cols)
    sides_at = cells_at + leaves * 4

    def seen_row(source, g, at):
        for p in range(0, cols, 4):
            start = cells_at + (g * cols + p) * 4
            four = source[start : start + 16].astype(F32)
            for k in range(4):
                lanes = slice(k % 2 * leaf, (k % 2 + 1) * leaf)
                window[at * broad + 1 + p + k] = four[k // 2 * 8 : (k // 2 + 1) * 8, lanes]
        two = source[sides_at : sides_at + 16].astype(F32)[:, g * leaf : (g + 1) * leaf]
        window[at * broad] = two[:8]
        window[(at + 1) * broad - 1] = two[8:]

    for g in range(rows):
        seen_row(own, g, g + 1)

    @pl.when(odd == 0)
    def _():
        seen_row(from_other, rows - 1, 0)
        seen_row(from_mate, 0, rows + 1)

    @pl.when(odd == 1)
    def _():
        seen_row(from_mate, rows - 1, 0)
        seen_row(from_other, 0, rows + 1)

    zero_cell = window.shape[0] - 1
    window[zero_cell] = jnp.zeros(window.shape[1:], F32)
    copies[0].wait()

    found = todo[0, todo.shape[1] - 1]

    def block_copy(at, n, slot):
        return pltpu.make_async_copy(
            far_blocks.at[at, n], blocks.at[slot], block_sems.at[slot]
        )

    def fetch(step, _):
        for k in range(4):
            slot = 4 * step + k

            @pl.when(slot < found)
            def _():
                pair = todo[0, slot]
                block_copy((pair >> 4) & 255, pair & 15, slot).start()

        return 0

    lax.fori_loop(0, (found + 3) // 4, fetch, 0)
    tables = (own, from_mate, from_other)
    copies[1].wait()
    leaf_pick = chosen(choose_leaf, tables, 0, leaves)
    copies[2].wait()
    pair_pick = chosen(choose_pair, tables, around * leaves, cols)
    split = bands * leaves
    copies[3].wait()
    fields[:split] = own_blocks(dot(leaf_pick, couple_leaf[...], NT), leaves)
    copies[4].wait()
    fields[split:] = own_blocks(dot(pair_pick, couple_pair[...], NT), cols)
    gathered[...] = local_part[...]

    def several(step, _):
        first = step * AT_ONCE
        for k in range(AT_ONCE):

            @pl.when(first + k < found)
            def _():
                block_copy(0, 0, first + k).wait()

        results = []
        for k in range(AT_ONCE):
            slot = jnp.minimum(first + k, found - 1)
            where = jnp.where(first + k < found, todo[0, slot] >> 12, zero_cell)
            cell = window[where].astype(BF16)
            if k % 2 == 0:
                results.append(dot(cell, blocks[slot], NT))
            else:
                results.append(dot(blocks[slot], cell, NT).T)
        for k in range(AT_ONCE):
            at = (todo[0, jnp.minimum(first + k, found - 1)] >> 4) & 255
            gathered[at] += results[k]
        return 0

    lax.fori_loop(0, (found + AT_ONCE - 1) // AT_ONCE, several, 0)


def result_kernel(
    tops, gathered, fields, choose_top, couple_top, basis, up_leaf, up_pair, emission, reflect, out
):
    bands, rows, cols, leaf = out.shape
    leaves = rows * cols
    picks = couple_top.shape[1] // RANK
    leaf_field = fields[: bands * leaves, :RANK]
    pair_field = fields[bands * leaves :, :RANK]
    size = tops.shape[0]
    top_pick = dot(choose_top[:, :size], tops[...], NN)
    upper = dot(choose_top[:, size:], tops[...], NN)
    top_pick = jnp.where(lax.broadcasted_iota(jnp.int32, upper.shape, 1) < RANK, top_pick, upper)
    top_pick = top_pick + pltpu.roll(top_pick, RANK, 1)
    top_pick = jnp.concatenate([top_pick] * (picks // 2), axis=1)
    kept = row_of(top_pick.shape, picks) == lax.broadcasted_iota(jnp.int32, top_pick.shape, 1) // RANK
    top_pick = jnp.where(kept, top_pick, 0.0).astype(BF16)
    top_field = dot(top_pick, couple_top[...], NT)
    top_field = jnp.sum(top_field.reshape(bands, picks, RANK), axis=1)
    spread = jnp.broadcast_to(top_field[:, None, :], (bands, cols, RANK))
    spread = spread.reshape(bands * cols, RANK).astype(BF16)
    pair_total = pair_field + own_blocks(dot(spread, up_pair[...], NT), cols)[:, :RANK]
    spread = jnp.broadcast_to(
        pair_total.reshape(bands, 1, cols, RANK), (bands, rows, cols, RANK)
    )
    spread = spread.reshape(bands * leaves, RANK).astype(BF16)
    leaf_total = leaf_field + own_blocks(dot(spread, up_leaf[...], NT), leaves)[:, :RANK]
    leaf_total = jnp.concatenate([leaf_total, leaf_total], axis=1)
    far_part = dot(on_diagonal(leaf_total, leaves), basis[...], NN)
    far_part = far_part.reshape(out.shape)
    for g in range(rows):
        near_part = jnp.swapaxes(gathered[g * cols : (g + 1) * cols], 0, 1)
        out[:, g] = emission[:, g] + reflect[:, g] * (near_part + far_part[:, g])


def body(
    radiosity,
    emission,
    reflect,
    basis,
    up_leaf,
    upward_pair_transfer,
    near_block,
    couple_leaf,
    couple_pair,
    couple_top,
    near_list,
    far_leaf,
    far_pair,
    far_top,
):
    around = lax.axis_size("perim")
    tall = lax.axis_size("section")
    bands, rows, cols, leaf = radiosity.shape
    leaves = rows * cols
    mates = [(s, s ^ 1) for s in range(tall)]
    others = [(s, s + 1 if s % 2 else s - 1) for s in range(1, tall - 1)]
    sems = pltpu.SemaphoreType.DMA
    basis = basis.reshape(leaves * RANK, leaf)
    up_leaf = up_leaf.reshape(leaves * RANK, RANK)
    up_pair = upward_pair_transfer.reshape(cols * RANK, RANK)
    sent, cells = pl.pallas_call(
        coefficients_kernel,
        out_shape=[
            pltpu.HBM((around, 16, WIDE), BF16),
            jax.ShapeDtypeStruct((leaves, bands, leaf), BF16),
        ],
        in_specs=[HBM] * 4,
        out_specs=[HBM, VMEM],
        scratch_shapes=[
            pltpu.VMEM(radiosity.shape, F32),
            pltpu.VMEM(basis.shape, BF16),
            pltpu.VMEM(up_leaf.shape, BF16),
            pltpu.VMEM(up_pair.shape, BF16),
            pltpu.VMEM((2, 16, WIDE), BF16),
            sems((around + 4,)),
        ],
        compiler_params=limit(4),
        name="coefficients",
    )(*map(far, [radiosity, basis, up_leaf, up_pair]))
    ring = lax.all_to_all(sent, "perim", 0, 0)
    blocks = near_block.reshape((leaves,) + near_block.shape[2:])
    couple_leaf = couple_leaf.reshape(leaves * RANK, -1)
    couple_pair = couple_pair.reshape(cols * RANK, -1)
    couple_top = couple_top[0, 0]
    listed = near_list.transpose(2, 0, 1)
    names_leaf = far_leaf.reshape(leaves, -1)
    names_pair = far_pair.reshape(cols, -1)
    names_top = far_top.reshape(1, -1)
    names = [names_leaf, names_pair, names_top]
    window = ((rows + 2) * (cols + 2), bands, leaf)
    choices = [
        pltpu.HBM((names_leaf.size, 3 * around * leaves), BF16),
        pltpu.HBM((names_pair.size, 3 * around * cols), BF16),
        pltpu.HBM((bands * names_top.size, tall * around * bands), BF16),
        pltpu.HBM((1, LANES), jnp.int32),
        jax.ShapeDtypeStruct((leaves, bands, leaf), F32),
    ]
    choose_leaf, choose_pair, choose_top, todo, local_part = pl.pallas_call(
        local_kernel,
        out_shape=choices,
        in_specs=[VMEM] + [HBM] * 5,
        out_specs=[HBM] * 4 + [VMEM],
        scratch_shapes=[
            pltpu.VMEM(window, F32),
            pltpu.SMEM(listed.shape, jnp.int32),
            pltpu.SMEM((1, LANES), jnp.int32),
        ]
        + [pltpu.VMEM(x.shape, x.dtype) for x in names + [blocks] + choices[:3]]
        + [sems((leaves + 9,))],
        compiler_params=limit(17),
        name="local",
    )(cells, *map(far, [listed] + names + [blocks]))
    packed = pl.pallas_call(
        packing_kernel,
        out_shape=jax.ShapeDtypeStruct((around * (leaves + cols) + leaves * 4 + 16, 512), BF16),
        in_specs=[VMEM, VMEM, ANY],
        out_specs=VMEM,
        compiler_params=limit(4),
        name="packing",
    )(ring, cells, local_part)
    tops = pl.pallas_call(
        tops_kernel,
        out_shape=pltpu.HBM((tall, around * bands // 2, LANES), BF16),
        in_specs=[VMEM],
        out_specs=HBM,
        scratch_shapes=[pltpu.VMEM((around * bands // 2, LANES), BF16), sems((tall,))],
        compiler_params=limit(3),
        name="tops",
    )(ring)
    from_mate = lax.ppermute(packed, "section", mates)
    from_other = lax.ppermute(packed, "section", others)
    tops = lax.all_to_all(tops, "section", 0, 0)
    most = leaves * (listed.shape[0] - 1)
    held = [choose_leaf, choose_pair, couple_leaf, couple_pair]
    gathered, fields = pl.pallas_call(
        field_kernel,
        out_shape=[
            jax.ShapeDtypeStruct((leaves, bands, leaf), F32),
            jax.ShapeDtypeStruct((bands * (leaves + cols), LANES), F32),
        ],
        in_specs=[VMEM] * 4 + [HBM] * 6,
        out_specs=[VMEM] * 2,
        scratch_shapes=[
            pltpu.VMEM((window[0] + 1,) + window[1:], F32),
            pltpu.SMEM(todo.shape, jnp.int32),
        ]
        + [pltpu.VMEM(x.shape, x.dtype) for x in held]
        + [pltpu.VMEM((most, leaf, leaf), BF16), sems((5,)), sems((most,))],
        compiler_params=limit(19),
        name="fields",
    )(
        packed,
        from_mate,
        from_other,
        local_part,
        *map(far, [todo] + held + [blocks]),
    )
    return pl.pallas_call(
        result_kernel,
        out_shape=jax.ShapeDtypeStruct(radiosity.shape, F32),
        in_specs=[VMEM] * 10,
        out_specs=VMEM,
        compiler_params=limit(4),
        name="result",
    )(
        tops.reshape(tall * around * bands // 2, LANES),
        gathered,
        fields,
        choose_top,
        couple_top,
        basis,
        up_leaf,
        up_pair,
        emission,
        reflect,
    )


def solution(mesh):
    cells = P(None, "section", "perim", None)
    four = P("section", "perim", None, None)
    lists = P("section", "perim", None)
    return jax.shard_map(
        body,
        mesh=mesh,
        in_specs=(cells,) * 3
        + (four,) * 3
        + (P("section", "perim", None, None, None),)
        + (four,) * 3
        + (lists,) * 4,
        out_specs=cells,
        check_vma=False,
    )
```
